32 devices in a mesh: space: 16 (over z, y, core), kgrp: 2 (over x).
Axes of the slice: x: 2, y: 2, z: 4, core: 2. Of those that a mesh axis runs over, the one named last changes fastest.
Arguments:
- features: bfloat16 [4096, 128], P(('space', 'kgrp')), may hold values from -8 to 8, as said below
- positions: float32 [4096, 3], P('space'), may hold values from 0 to 512, as said below
- wave_index: int32 [1536, 3], P('kgrp'), may hold values from -12 to 12, as said below
- wave_filter: float32 [1536, 128], P('kgrp'), may hold values from 0.2 to 2
- mix_pair: bfloat16 [2, 128, 128], replicated, may hold values from -0.5 to 0.5
- msg_weight: bfloat16 [128, 128], replicated, may hold values from -0.5 to 0.5
- chan_width: float32 [128], replicated, may hold values from 1 to 30
- pair_dist: float32 [4096, 16], P(('space', 'kgrp')), may hold values from 1 to 25
- neighbours: int32 [4096, 16], P(('space', 'kgrp')), may hold values from 0 to 191, as said below
- norm_gain: float32 [128], replicated, may hold values from 0.1 to 1.9
- in_weight: bfloat16 [128, 512], replicated, may hold values from -0.5 to 0.5
- out_weight: bfloat16 [512, 128], replicated, may hold values from -0.25 to 0.25
Outputs:
- updated: bfloat16 [4096, 128], P(('space', 'kgrp'))
The draws below stay inside these ranges and needn't reach their ends.
Inputs may be any that keep to these rules, and one draw needn't show every extreme that they name: Entries of the features are clipped to the range. `positions`: x and y lie in [0, 16); atom i has z in [i / 8, (i + 1) / 8). `wave_index`: the wave vectors are distinct and nonzero, one of each plus-minus k pair: each is lexicographically positive (first nonzero component positive). Rows of a device's extended block are its lower 32 wrapped neighbours' rows, its own 128 rows, then 32 upper ones; an atom at own row r lists rows r + 32 + o with 1 <= |o| <= 32.
All inputs are finite; a program needn't handle non-finite values.
Results may differ from the reference program's by a relative error of at most 0.008.
Values may be sent and summed in bfloat16 or wider, within the bound.
No kernel may reach another device: no remote copies, remote signals or barrier semaphores. Data moves between devices by JAX's collectives and lax.ppermute only.
A program may use at most 64 MiB of HBM per device.

```python
import math
import jax
import jax.numpy as jnp
from jax import lax

F = 128
H = 512
NB = 16
KMAX = 12
ATOM_DEV = 128
ATOMS = 4096
WAVES = 1536
N_SPACE = 16
N_KGRP = 2


def draw_features(key, part):
    key_base, key_rows, key_cols = jax.random.split(key, 3)
    row_scale = jnp.exp(jax.random.uniform(key_rows, (ATOMS, 1), minval=math.log(0.3), maxval=math.log(3.0)))
    col_scale = jnp.exp(jax.random.uniform(key_cols, (1, F), minval=math.log(0.5), maxval=math.log(2.0)))
    base = jax.random.normal(key_base, (ATOMS, F))
    return jnp.clip(base * row_scale * col_scale, -8.0, 8.0).astype(jnp.bfloat16)


def draw_positions(key, part):
    key_plane, key_depth = jax.random.split(key, 2)
    plane = jax.random.uniform(key_plane, (ATOMS, 2), minval=0.0, maxval=16.0)
    order = jnp.arange(ATOMS, dtype=jnp.int32).astype(jnp.float32)
    depth = (order + jax.random.uniform(key_depth, (ATOMS,), minval=0.0, maxval=0.999)) * 0.125
    return jnp.concatenate([plane, depth[:, None]], axis=1).astype(jnp.float32)


def draw_wave_index(key, part):
    side = 2 * KMAX + 1
    centre = (side * side * side - 1) // 2
    chosen = jax.random.permutation(jax.random.fold_in(key, 71), centre)[:WAVES].astype(jnp.int32) + centre + 1
    first = chosen // (side * side) - KMAX
    second = chosen // side % side - KMAX
    third = chosen % side - KMAX
    return jnp.stack([first, second, third], axis=1).astype(jnp.int32)


def draw_neighbours(key, part):
    halo_width = ATOM_DEV // 4
    key_reach, key_side = jax.random.split(key, 2)
    reach = jax.random.randint(key_reach, (ATOMS, NB), 1, halo_width + 1)
    side = jax.random.randint(key_side, (ATOMS, NB), 0, 2) * 2 - 1
    offset = reach * side
    local = (jnp.arange(ATOMS, dtype=jnp.int32) % ATOM_DEV)[:, None]
    slot = jnp.arange(NB, dtype=jnp.int32)[None, :]
    offset = jnp.where((local == 0) & (slot == 0), -halo_width, offset)
    offset = jnp.where((local == ATOM_DEV - 1) & (slot == 0), halo_width, offset)
    return (local + halo_width + offset).astype(jnp.int32)


def levels(stream_key, extent, pieces, low, top_value):
    def one(position, shards_of):
        draws = jax.random.uniform(jax.random.fold_in(jax.random.fold_in(stream_key, 6), position), (shards_of,), jnp.float32, low / len(pieces), top_value / len(pieces))
        return jnp.repeat(jnp.exp(draws), extent[position] // shards_of).reshape((-1,) + (1,) * (len(extent) - position - 1))

    factor_of = one(*pieces[0])
    for cut in pieces[1:]:
        factor_of = factor_of * one(*cut)
    return factor_of


def scatter_about(own_key, shape, deviation, bound, held_as=jnp.bfloat16):
    values = deviation * jax.random.normal(own_key, shape, jnp.float32)
    return jnp.clip(values, min=-bound, max=bound).astype(held_as)


def setup_inputs(seed: int = 0) -> dict:
    seeds = jax.random.split(jax.random.key(seed), 13)
    return {
        "features": draw_features(jax.random.fold_in(seeds[12], 71), 0),
        "positions": draw_positions(jax.random.fold_in(seeds[12], 71), 0),
        "wave_index": draw_wave_index(jax.random.fold_in(seeds[12], 71), 0),
        "wave_filter": jnp.clip(jnp.exp(math.log(2.0) - 2.3025851 * jax.random.uniform(seeds[3], (WAVES, F), jnp.float32) ** levels(seeds[3], (WAVES, F), ((0, 2),), -0.2, 0.2)), 0.2, 2.0),
        "mix_pair": scatter_about(seeds[4], (2, F, F), F ** -0.5, 0.5),
        "msg_weight": scatter_about(seeds[5], (F, F), F ** -0.5, 0.5),
        "chan_width": jnp.clip(jnp.exp(jax.random.uniform(seeds[6], (F,), jnp.float32, math.log(1.0), math.log(30.0))), 1.0, 30.0),
        "pair_dist": jnp.clip(1.0 + 24.0 * jax.random.uniform(seeds[7], (ATOMS, NB), jnp.float32) ** levels(seeds[7], (ATOMS, NB), ((0, 32),), -0.2, 0.2), 1.0, 25.0),
        "neighbours": draw_neighbours(jax.random.fold_in(seeds[12], 71), 0),
        "norm_gain": jnp.clip(1.0 + 0.18 * jax.random.normal(seeds[9], (F,), jnp.float32), 0.1, 1.9),
        "in_weight": scatter_about(seeds[10], (F, H), F ** -0.5, 0.5),
        "out_weight": scatter_about(seeds[11], (H, F), H ** -0.5, 0.25),
    }


box_side = 16.0
slab_step = 0.125
two_pi = 2.0 * math.pi

def wave_vectors(wave_index, slab_length):
    counts = wave_index.astype(jnp.float32)
    return jnp.stack([counts[:, 0] * (two_pi / box_side), counts[:, 1] * (two_pi / box_side), counts[:, 2] * (two_pi / slab_length)], axis=0)

def phase_angles(points, wave_vecs):
    return points[:, 0:1] * wave_vecs[0:1, :] + points[:, 1:2] * wave_vecs[1:2, :] + points[:, 2:3] * wave_vecs[2:3, :]

def mix_vectors(s_re, s_im, mix_pair, wave_filter, scale):
    a_re = (s_re * scale).astype(jnp.bfloat16)
    a_im = (s_im * scale).astype(jnp.bfloat16)
    real_real = jnp.dot(a_re, mix_pair[0], preferred_element_type=jnp.float32)
    imag_imag = jnp.dot(a_im, mix_pair[1], preferred_element_type=jnp.float32)
    real_imag = jnp.dot(a_re, mix_pair[1], preferred_element_type=jnp.float32)
    imag_real = jnp.dot(a_im, mix_pair[0], preferred_element_type=jnp.float32)
    y_re = (wave_filter * (real_real - imag_imag)).astype(jnp.bfloat16)
    y_im = (wave_filter * (real_imag + imag_real)).astype(jnp.bfloat16)
    return (y_re, y_im)

def wave_terms(points, wave_vecs, y_re, y_im, inv_scale):
    angles = phase_angles(points, wave_vecs)
    cos_part = jnp.cos(angles).astype(jnp.bfloat16)
    sin_part = jnp.sin(angles).astype(jnp.bfloat16)
    summed = jnp.dot(cos_part, y_re, preferred_element_type=jnp.float32) + jnp.dot(sin_part, y_im, preferred_element_type=jnp.float32)
    return summed * inv_scale

def reference(features, positions, wave_index, wave_filter, mix_pair, msg_weight, chan_width, pair_dist, neighbours, norm_gain, in_weight, out_weight):
    domain = ATOM_DEV * N_KGRP
    halo_width = ATOM_DEV // 4
    projected = jnp.dot(features, msg_weight, preferred_element_type=jnp.float32).astype(jnp.bfloat16)
    row_ids = jnp.arange(ATOMS, dtype=jnp.int32).reshape(N_SPACE, domain)

    def domain_message(block):
        ids, nbr_block, dist_block = block
        local = ids % ATOM_DEV
        source = (ids[:, None] - local[:, None] + nbr_block - halo_width) % ATOMS
        nearby = jnp.take(projected, source.astype(jnp.int32), axis=0)
        weights = jnp.exp(-dist_block[:, :, None] / chan_width[None, None, :])
        return lax.optimization_barrier(jnp.sum(weights * nearby.astype(jnp.float32), axis=1))
    message = lax.map(domain_message, (row_ids, neighbours.reshape(N_SPACE, domain, NB), pair_dist.reshape(N_SPACE, domain, NB))).reshape(ATOMS, F)
    wave_vecs = wave_vectors(wave_index, ATOMS * slab_step)
    feat_blocks = features.reshape(N_SPACE, domain, F)
    pos_blocks = positions.reshape(N_SPACE, domain, 3)
    dims = (((0,), (0,)), ((), ()))

    def add_domain(carry, block):
        feat_block, pos_block = block
        angles = phase_angles(pos_block, wave_vecs)
        cos_part = jnp.cos(angles).astype(jnp.bfloat16)
        sin_part = jnp.sin(angles).astype(jnp.bfloat16)
        new_re = carry[0] + lax.dot_general(cos_part, feat_block, dims, preferred_element_type=jnp.float32)
        new_im = carry[1] + lax.dot_general(sin_part, feat_block, dims, preferred_element_type=jnp.float32)
        return ((new_re, new_im), None)
    zeros = jnp.zeros((WAVES, F), jnp.float32)
    (s_re, s_im), _ = lax.scan(add_domain, (zeros, zeros), (feat_blocks, pos_blocks))
    y_re, y_im = mix_vectors(s_re, s_im, mix_pair, wave_filter, 1.0 / math.sqrt(ATOMS))
    inv_scale = 1.0 / math.sqrt(WAVES)
    ewald = lax.map(lambda pos_block: wave_terms(pos_block, wave_vecs, y_re, y_im, inv_scale), pos_blocks).reshape(ATOMS, F)
    mixed = features.astype(jnp.float32) + message + ewald
    inverse = lax.rsqrt(lax.optimization_barrier(jnp.mean(mixed * mixed, axis=1, keepdims=True)) + 1e-06)
    normed = (mixed * inverse * norm_gain).astype(jnp.bfloat16)
    hidden = jax.nn.silu(jnp.dot(normed, in_weight, preferred_element_type=jnp.float32)).astype(jnp.bfloat16)
    return (mixed + jnp.dot(hidden, out_weight, preferred_element_type=jnp.float32)).astype(jnp.bfloat16)
```

```python
import functools
import math

import jax
import jax.numpy as jnp
import numpy as np
from jax import lax
from jax.experimental import pallas as pl
from jax.experimental.pallas import tpu as pltpu
from jax.sharding import PartitionSpec as P

box_side = 16.0
slab_step = 0.125
coord_rows = 16
bf16, f32 = jnp.bfloat16, jnp.float32

both = ("space", "kgrp")

def fit_cosine(degree):
    count = 64
    theta = (np.arange(count) + 0.5) * math.pi / count
    u = 0.125 * (1.0 + np.cos(theta))
    values = np.cos(2.0 * math.pi * np.sqrt(u))
    cheb = np.polynomial.chebyshev.Chebyshev.fit(u, values, degree, domain=[0.0, 0.25])
    return [float(c) for c in cheb.convert(kind=np.polynomial.Polynomial).coef]


cosine = fit_cosine(6)


def dot(a, b, dims):
    return lax.dot_general(a, b, (dims, ((), ())), preferred_element_type=f32)


def whole(count):
    return [pl.BlockSpec(memory_space=pltpu.VMEM)] * count


def call(body, outs, *args, flops=0, transcendentals=0):
    moved = sum(a.size * a.dtype.itemsize for a in (*args, *outs))
    return pl.pallas_call(
        body,
        out_shape=outs if len(outs) > 1 else outs[0],
        in_specs=whole(len(args)),
        out_specs=whole(len(outs)) if len(outs) > 1 else whole(1)[0],
        cost_estimate=pl.CostEstimate(
            flops=flops, bytes_accessed=moved, transcendentals=transcendentals
        ),
        compiler_params=pltpu.CompilerParams(vmem_limit_bytes=24 * 1024 * 1024),
    )(*args)


def shape(dims, dtype):
    return jax.ShapeDtypeStruct(dims, dtype)


def payload_body(slab_length, feat_ref, pos_ref, out_ref):
    atoms = feat_ref.shape[0]
    group = lax.axis_index("kgrp")
    out_ref[:atoms, :] = feat_ref[...]
    own = pos_ref[:, pl.ds(pl.multiple_of(group * atoms, atoms), atoms)]
    row = lax.broadcasted_iota(jnp.int32, own.shape, 0)
    turns = own * jnp.where(row == 2, 1.0 / slab_length, 1.0 / box_side)
    high = turns.astype(bf16).astype(f32)
    rest = turns - high
    middle = rest.astype(bf16).astype(f32)
    low = rest - middle
    ones = jnp.ones((1, atoms), f32)
    zeros = jnp.zeros((coord_rows - 10, atoms), f32)
    parts = jnp.concatenate([high, middle, low, ones, zeros], axis=0)
    out_ref[atoms:, :] = parts.astype(bf16)


def structure_body(blocks, carried, *refs):
    block_refs, (wave_ref, *refs) = refs[:blocks], refs[blocks:]
    carry_ref = None
    if carried:
        carry_ref, *refs = refs
    phase_ref, sum_ref = refs
    atoms = block_refs[0].shape[0] - coord_rows
    total = None if carry_ref is None else carry_ref[...]
    for i, ref in enumerate(block_refs):
        turns = dot(ref[atoms:, :], wave_ref[...], ((0,), (0,)))
        part = turns - jnp.round(turns)
        u = part * part
        value = jnp.full_like(u, cosine[-1])
        for c in cosine[-2::-1]:
            value = value * u + c
        phase = value.astype(bf16)
        phase_ref[i * atoms : (i + 1) * atoms, :] = phase
        term = dot(ref[:atoms, :], phase, ((0,), (0,)))
        total = term if total is None else total + term
    sum_ref[...] = total.astype(sum_ref.dtype)


def structure(blocks, waves, carry):
    atoms, channels = blocks[0].shape[0] - coord_rows, blocks[0].shape[1]
    columns = waves.shape[1]
    outs = (
        shape((len(blocks) * atoms, columns), bf16),
        shape((channels, columns), f32 if carry is None else bf16),
    )
    extra = () if carry is None else (carry,)
    work = len(blocks) * atoms * columns
    return call(
        functools.partial(structure_body, len(blocks), carry is not None),
        outs,
        *blocks,
        waves,
        *extra,
        flops=2 * work * (channels + coord_rows) + 16 * work,
    )


def ewald_body(scale, inv_scale, a_ref, b_ref, mix_ref, filter_ref, near_ref, far_ref, keep_ref, send_ref):
    total = (a_ref[...].astype(f32) + b_ref[...].astype(f32)) * scale
    amps = total.astype(bf16)
    columns = amps.shape[1]
    straight = dot(mix_ref[0], amps, ((0,), (0,)))
    crossed = dot(mix_ref[1], amps, ((0,), (0,)))
    half = columns // 2
    crossed = jnp.concatenate([-crossed[:, half:], crossed[:, :half]], axis=1)
    y = (filter_ref[...] * (straight + crossed)).astype(bf16)
    send_ref[...] = (dot(far_ref[...], y, ((1,), (1,))) * inv_scale).astype(bf16)
    keep_ref[...] = dot(near_ref[...], y, ((1,), (1,))) * inv_scale


def message_body(feat_ref, before_ref, after_ref, msg_ref, width_ref, dist_ref, nbr_ref, base_ref):
    atoms = feat_ref.shape[0]
    extended = jnp.concatenate([before_ref[...], feat_ref[...], after_ref[...]], axis=0)
    projected = dot(msg_ref[...], extended, ((0,), (1,))).astype(bf16)
    rows = extended.shape[0]
    row = lax.broadcasted_iota(jnp.int32, (rows, atoms), 0)
    inverse = -1.0 / width_ref[...]
    message = jnp.zeros((projected.shape[0], atoms), f32)
    for j in range(nbr_ref.shape[0]):
        chosen = jnp.where(row == nbr_ref[j : j + 1, :], 1.0, 0.0).astype(bf16)
        nearby = dot(projected, chosen, ((1,), (0,)))
        message = message + jnp.exp(dist_ref[j : j + 1, :] * inverse) * nearby
    base_ref[...] = feat_ref[...].astype(f32) + message.T


def final_body(peers, *refs):
    base_ref, *refs = refs
    peer_refs, (gain_ref, in_ref, out_ref, result_ref) = refs[:peers], refs[peers:]
    mixed = base_ref[...]
    for ref in peer_refs:
        mixed = mixed + ref[...].astype(f32)
    inverse = lax.rsqrt(jnp.mean(mixed * mixed, axis=1, keepdims=True) + 1e-06)
    normed = (mixed * inverse * gain_ref[...]).astype(bf16)
    hidden = dot(normed, in_ref[...], ((1,), (0,)))
    hidden = (hidden * (1.0 / (1.0 + jnp.exp(-hidden)))).astype(bf16)
    result_ref[...] = (mixed + dot(hidden, out_ref[...], ((1,), (0,)))).astype(bf16)


def local(
    outer,
    features,
    positions,
    wave_index,
    wave_filter,
    mix_pair,
    msg_weight,
    chan_width,
    pair_dist,
    neighbours,
    norm_gain,
    in_weight,
    out_weight,
):
    atoms, channels = features.shape
    groups, space = lax.axis_size("kgrp"), lax.axis_size("space")
    inner = space // outer
    members = inner * groups
    devices = space * groups
    total_atoms = atoms * devices
    halo = atoms // 4
    slab_length = total_atoms * slab_step
    own_space = lax.axis_index("space")
    member = (own_space * groups + lax.axis_index("kgrp")) % members

    def swap(x, mask):
        return lax.ppermute(x, both, [(i, i ^ mask) for i in range(devices)])

    near = [m for m in range(members) if not m & groups]
    sent = call(
        functools.partial(payload_body, slab_length),
        (shape((atoms + coord_rows, channels), bf16),),
        features,
        positions.T,
    )
    near_blocks = [sent] + [swap(sent, m) for m in near[1:]]
    far_blocks = [swap(block, groups) for block in near_blocks]
    of_mask = {m: b for m, b in zip(near, near_blocks)}
    of_mask.update({m ^ groups: b for m, b in zip(near, far_blocks)})

    share = wave_index.shape[0] // inner
    first = (own_space % inner) * share
    counts = lax.dynamic_slice_in_dim(wave_index.T, first, share, 1).astype(f32)
    counts = jnp.concatenate([counts, counts], axis=1)
    quarter = jnp.where(jnp.arange(2 * share)[None, :] < share, 0.0, -0.25)
    zeros = jnp.zeros((coord_rows - 10, 2 * share), f32)
    waves = jnp.concatenate([counts, counts, counts, quarter, zeros], axis=0).astype(bf16)
    filters = lax.dynamic_slice_in_dim(wave_filter, first, share, 0).T
    filters = jnp.concatenate([filters, filters], axis=1)

    near_phase, near_sum = structure(near_blocks, waves, None)
    far_phase, amps = structure(far_blocks, waves, near_sum)

    step = 1
    while 2 * step < outer:
        other = swap(amps, (2 * step - 1) * members)
        amps = (amps.astype(f32) + other.astype(f32)).astype(bf16)
        step *= 2
    if outer > 1:
        other = swap(amps, (2 * step - 1) * members)
    else:
        other = jnp.zeros_like(amps)

    columns = 2 * share
    half = len(near) * atoms
    keep, send = call(
        functools.partial(
            ewald_body, 1.0 / math.sqrt(total_atoms), 1.0 / math.sqrt(wave_index.shape[0] * groups)
        ),
        (shape((half, channels), f32), shape((half, channels), bf16)),
        amps,
        other,
        mix_pair,
        filters,
        near_phase,
        far_phase,
        flops=2 * channels * columns * (2 * channels + 2 * half),
    )
    came = swap(send, groups)
    terms = keep + came.astype(f32)
    peers = [terms[:atoms]]
    for i, m in enumerate(near[1:], 1):
        peers.append(swap(terms[i * atoms : (i + 1) * atoms].astype(bf16), m))

    edge = jnp.where(member == 0, features[:halo], features[atoms - halo :])
    pairs = []
    for layer in range(outer):
        above = (layer + 1) % outer
        pairs.append((layer * members + members - 1, above * members))
        pairs.append((above * members, layer * members + members - 1))
    before = after = lax.ppermute(edge, both, pairs)
    mask = 1
    while mask < members:
        block = of_mask[mask]
        span = (mask + 1) // 2
        before = jnp.where(member % (2 * span) == span, block[atoms - halo : atoms], before)
        after = jnp.where((member + 1) % (2 * span) == span, block[:halo], after)
        mask = 2 * mask + 1
    slots = neighbours.shape[1]
    base = call(
        message_body,
        (shape((atoms, channels), f32),),
        features,
        before,
        after,
        msg_weight,
        chan_width.reshape(channels, 1),
        pair_dist.T,
        neighbours.T,
        flops=2 * channels * atoms * slots * (atoms + 2 * halo),
        transcendentals=atoms * slots * channels,
    )
    return call(
        functools.partial(final_body, len(peers)),
        (shape((atoms, channels), bf16),),
        base,
        *peers,
        norm_gain.reshape(1, channels),
        in_weight,
        out_weight,
        flops=4 * atoms * channels * in_weight.shape[1],
    )


def layers(mesh):
    depths = {getattr(d, "coords", (0, 0, i))[2] for i, d in enumerate(mesh.devices[:, 0])}
    return len(depths)


def solution(mesh):
    placed = (
        P(both, None),
        P("space", None),
        P("kgrp", None),
        P("kgrp", None),
        P(),
        P(),
        P(),
        P(both, None),
        P(both, None),
        P(),
        P(),
        P(),
    )
    return jax.shard_map(
        functools.partial(local, layers(mesh)),
        mesh=mesh,
        in_specs=placed,
        out_specs=P(both, None),
        check_vma=False,
    )
```

```python
import functools
import math

import jax
import jax.numpy as jnp
import numpy as np
from jax import lax
from jax.experimental import pallas as pl
from jax.experimental.pallas import tpu as pltpu
from jax.sharding import PartitionSpec as P

box_side = 16.0
slab_step = 0.125
coord_rows = 16
bf16, f32 = jnp.bfloat16, jnp.float32

both = ("space", "kgrp")

vector_flops = 15000

def fit_cosine(degree):
    count = 64
    theta = (np.arange(count) + 0.5) * math.pi / count
    u = 0.125 * (1.0 + np.cos(theta))
    values = np.cos(2.0 * math.pi * np.sqrt(u))
    cheb = np.polynomial.chebyshev.Chebyshev.fit(u, values, degree, domain=[0.0, 0.25])
    return [float(c) for c in cheb.convert(kind=np.polynomial.Polynomial).coef]


cosine = fit_cosine(6)


def dot(a, b, dims):
    return lax.dot_general(a, b, (dims, ((), ())), preferred_element_type=f32)


def whole(count):
    return [pl.BlockSpec(memory_space=pltpu.VMEM)] * count


def call(body, outs, *args, flops=0, transcendentals=0):
    moved = sum(a.size * a.dtype.itemsize for a in (*args, *outs))
    return pl.pallas_call(
        body,
        out_shape=outs if len(outs) > 1 else outs[0],
        in_specs=whole(len(args)),
        out_specs=whole(len(outs)) if len(outs) > 1 else whole(1)[0],
        cost_estimate=pl.CostEstimate(
            flops=flops, bytes_accessed=moved, transcendentals=transcendentals
        ),
        compiler_params=pltpu.CompilerParams(vmem_limit_bytes=24 * 1024 * 1024),
    )(*args)


def shape(dims, dtype):
    return jax.ShapeDtypeStruct(dims, dtype)


def coordinate_parts(coords, slab_length):
    atoms = coords.shape[1]
    row = lax.broadcasted_iota(jnp.int32, coords.shape, 0)
    turns = coords * jnp.where(row == 2, 1.0 / slab_length, 1.0 / box_side)
    high = turns.astype(bf16).astype(f32)
    rest = turns - high
    middle = rest.astype(bf16).astype(f32)
    low = rest - middle
    ones = jnp.ones((1, atoms), f32)
    zeros = jnp.zeros((coord_rows - 10, atoms), f32)
    return jnp.concatenate([high, middle, low, ones, zeros], axis=0).astype(bf16)


def cosines(turns):
    part = turns - jnp.round(turns)
    u = part * part
    value = jnp.full_like(u, cosine[-1])
    for c in cosine[-2::-1]:
        value = value * u + c
    return value.astype(bf16)


def fill_phases(coord_refs, waves, groups, slab_length, phase_ref):
    group = lax.axis_index("kgrp")
    atoms = coord_refs[0].shape[1] // groups
    for i in range(len(coord_refs) * groups):
        start = pl.multiple_of((group ^ (i % groups)) * atoms, atoms)
        parts = coordinate_parts(coord_refs[i // groups][:, pl.ds(start, atoms)], slab_length)
        phase_ref[i * atoms : (i + 1) * atoms, :] = cosines(dot(parts, waves, ((0,), (0,))))


def quarter_body(out_ref):
    share = out_ref.shape[1] // 2
    row = lax.broadcasted_iota(jnp.int32, out_ref.shape, 0)
    column = lax.broadcasted_iota(jnp.int32, out_ref.shape, 1)
    out_ref[...] = jnp.where((row == 9) & (column >= share), -0.25, 0.0)


def prepare_body(inner, groups, slab_length, quarter_ref, index_ref, pos_ref, wave_ref, phase_ref):
    share = index_ref.shape[1] // inner
    first = lax.axis_index("space") & (inner - 1)
    counts = index_ref[...].astype(f32)
    mine = counts[:, :share]
    for i in range(1, inner):
        mine = jnp.where(first == i, counts[:, i * share : (i + 1) * share], mine)
    counts = jnp.concatenate([mine, mine], axis=1)
    zeros = jnp.zeros((coord_rows - 9, 2 * share), f32)
    waves = jnp.concatenate([counts, counts, counts, zeros], axis=0) + quarter_ref[...]
    wave_ref[...] = waves.astype(bf16)
    fill_phases([pos_ref], wave_ref[...], groups, slab_length, phase_ref)


def phase_body(groups, slab_length, *refs):
    *coord_refs, wave_ref, phase_ref = refs
    fill_phases(coord_refs, wave_ref[...], groups, slab_length, phase_ref)


def phases(coords, waves, groups, slab_length):
    rows = len(coords) * coords[0].shape[1]
    return call(
        functools.partial(phase_body, groups, slab_length),
        (shape((rows, waves.shape[1]), bf16),),
        *coords,
        waves,
        flops=vector_flops * rows * waves.shape[1],
    )


def layer_member(members):
    member = lax.axis_index("space") * lax.axis_size("kgrp") + lax.axis_index("kgrp")
    return member & (members - 1)


def structure_body(count, places, phases, members, atoms, final, *refs):
    block_refs, refs = refs[:count], refs[count:]
    phase_refs, (*carry_refs, sum_ref) = refs[:phases], refs[phases:]
    channels = block_refs[0].shape[1]
    total = carry_refs[0][...] if carry_refs else None
    blocks = [
        ref[i : i + atoms, :] for ref in block_refs for i in range(0, ref.shape[0], atoms)
    ]
    for block, (which, at) in zip(blocks, places):
        phase = phase_refs[which][at * atoms : (at + 1) * atoms, :]
        term = dot(block, phase, ((0,), (0,)))
        total = term if total is None else total + term
    sum_ref[:channels, :] = total.astype(sum_ref.dtype)
    if final:
        last = blocks[-1]
        halo = atoms // 4
        first = layer_member(members) == 0
        edge = jnp.where(first, last[atoms - halo :, :], last[:halo, :])
        sum_ref[channels:, :] = jnp.zeros_like(sum_ref[channels:, :])
        for r, c, piece in edge_places(halo, channels, sum_ref.shape[1]):
            sum_ref[channels + r : channels + r + 16, c : c + channels] = edge[piece : piece + 16]


def edge_places(halo, channels, columns):
    per_row = columns // channels
    return [
        (i // per_row * 16, i % per_row * channels, i * 16) for i in range(halo // 16)
    ]


def structure(blocks, places, phases, carry, members, atoms, final):
    channels = blocks[0].shape[1]
    columns = phases[0].shape[1]
    if final:
        edges = edge_places(atoms // 4, channels, columns)
        out = shape((channels + edges[-1][0] + 16, columns), bf16)
    else:
        out = shape((channels, columns), f32)
    extra = () if carry is None else (carry,)
    return call(
        functools.partial(structure_body, len(blocks), places, len(phases), members, atoms, final),
        (out,),
        *blocks,
        *phases,
        *extra,
        flops=2 * len(places) * atoms * columns * channels,
    )


def ewald_body(scale, inv_scale, places, phases, a_ref, b_ref, mix_ref, filter_ref, *refs):
    phase_refs, out_refs = refs[:phases], refs[phases:]
    channels = mix_ref.shape[1]
    total = (a_ref[:channels, :].astype(f32) + b_ref[:channels, :].astype(f32)) * scale
    amps = total.astype(bf16)
    columns = amps.shape[1]
    straight = dot(mix_ref[0], amps, ((0,), (0,)))
    crossed = dot(mix_ref[1], amps, ((0,), (0,)))
    half = columns // 2
    crossed = jnp.concatenate([-crossed[:, half:], crossed[:, :half]], axis=1)
    y = (filter_ref[...] * (straight + crossed)).astype(bf16)
    for ref, blocks in zip(out_refs, places):
        rows = ref.shape[0] // len(blocks)
        for i, (which, at) in enumerate(blocks):
            phase = phase_refs[which][at * rows : (at + 1) * rows, :]
            term = dot(phase, y, ((1,), (1,))) * inv_scale
            ref[i * rows : (i + 1) * rows, :] = term.astype(ref.dtype)


def halo_rows(members, blocks, stage_refs):
    atoms, channels = blocks[0].shape
    halo = atoms // 4
    member = layer_member(members)
    layer = lax.axis_index("space") // (members // lax.axis_size("kgrp"))
    before, after = blocks[-1][atoms - halo :, :], blocks[-1][:halo, :]
    places = edge_places(halo, channels, stage_refs[0].shape[1]) if stage_refs else []
    for i, ref in enumerate(stage_refs):
        edge = jnp.concatenate(
            [ref[channels + r : channels + r + 16, c : c + channels] for r, c, _ in places], axis=0
        )
        if i == 0:
            before = after = edge
        else:
            before = jnp.where((layer & ((1 << i) - 1)) == 0, edge, before)
            after = jnp.where(((layer + 1) & ((1 << i) - 1)) == 0, edge, after)
    for i, block in enumerate(blocks):
        span = 1 << i
        before = jnp.where((member & (2 * span - 1)) == span, block[atoms - halo :, :], before)
        after = jnp.where(((member + 1) & (2 * span - 1)) == span, block[:halo, :], after)
    return before, after


def message_body(members, places, refs_of_blocks, *refs):
    block_refs, refs = refs[:refs_of_blocks], refs[refs_of_blocks:]
    *stage_refs, msg_ref, width_ref, dist_ref, nbr_ref, base_ref = refs
    feat_ref = block_refs[0]
    channels, atoms = feat_ref.shape[1], dist_ref.shape[1]
    blocks = [block_refs[which][row : row + atoms, :] for which, row in places]
    before, after = halo_rows(members, blocks, stage_refs)
    extended = jnp.concatenate([before, feat_ref[:atoms, :], after], axis=0)
    projected = dot(msg_ref[...], extended, ((0,), (1,))).astype(bf16)
    rows = extended.shape[0]
    row = lax.broadcasted_iota(jnp.int32, (rows, atoms), 0)
    inverse = -1.0 / jnp.broadcast_to(width_ref[...], (atoms, channels)).T
    message = jnp.zeros((projected.shape[0], atoms), f32)
    for j in range(nbr_ref.shape[0]):
        chosen = jnp.where(row == nbr_ref[j : j + 1, :], 1.0, 0.0).astype(bf16)
        nearby = dot(projected, chosen, ((1,), (0,)))
        message = message + jnp.exp(dist_ref[j : j + 1, :] * inverse) * nearby
    base_ref[...] = feat_ref[:atoms, :].astype(f32) + message.T


def final_body(peers, *refs):
    base_ref, *refs = refs
    peer_refs, (gain_ref, in_ref, out_ref, result_ref) = refs[:peers], refs[peers:]
    mixed = base_ref[...]
    for ref in peer_refs:
        mixed = mixed + ref[...].astype(f32)
    inverse = lax.rsqrt(jnp.mean(mixed * mixed, axis=1, keepdims=True) + 1e-06)
    normed = (mixed * inverse * gain_ref[...]).astype(bf16)
    hidden = dot(normed, in_ref[...], ((1,), (0,)))
    hidden = (hidden * (1.0 / (1.0 + jnp.exp(-hidden)))).astype(bf16)
    result_ref[...] = (mixed + dot(hidden, out_ref[...], ((1,), (0,)))).astype(bf16)


def local(
    outer,
    features,
    positions,
    wave_index,
    wave_filter,
    mix_pair,
    msg_weight,
    chan_width,
    pair_dist,
    neighbours,
    norm_gain,
    in_weight,
    out_weight,
):
    atoms, channels = features.shape
    groups, space = lax.axis_size("kgrp"), lax.axis_size("space")
    inner = space // outer
    members = inner * groups
    devices = space * groups
    total_atoms = atoms * devices
    slab_length = total_atoms * slab_step

    def swap(x, mask):
        return lax.ppermute(x, both, [(i, i ^ mask) for i in range(devices)])

    near = [m for m in range(members) if not m & groups]
    single = [m for m in near if m & (m - 1) == 0]
    direct = [m for m in near if m not in single]
    bases = [m for m in near if m % groups == 0]
    block = {0: features}
    coords = {0: positions.T}
    for m in near[1:]:
        block[m] = swap(features, m)
    for m in bases[1:]:
        coords[m] = swap(positions.T, m)
    share = wave_index.shape[0] // inner
    quarter = call(quarter_body, (shape((coord_rows, 2 * share), f32),))
    waves, own_phase = call(
        functools.partial(prepare_body, inner, groups, slab_length),
        (shape((coord_rows, 2 * share), bf16), shape((groups * atoms, 2 * share), bf16)),
        quarter,
        wave_index.T,
        coords[0],
        flops=vector_flops * 2 * groups * atoms * share,
    )
    first = (lax.axis_index("space") % inner) * share
    filters = lax.dynamic_slice_in_dim(wave_filter, first, share, 0).T
    filters = jnp.concatenate([filters, filters], axis=1)
    far_blocks = swap(jnp.concatenate([block[m] for m in near], axis=0), groups)
    far_at = {m ^ groups: i * atoms for i, m in enumerate(near)}
    crossed = swap(jnp.concatenate([coords[m] for m in bases], axis=1), groups)
    own = groups * atoms
    for i, m in enumerate(bases):
        coords[m ^ groups] = crossed[:, i * own : (i + 1) * own]
    early = phases([coords[m] for m in bases[1:]], waves, groups, slab_length)
    late = phases([coords[m ^ groups] for m in bases], waves, groups, slab_length)
    phase = [own_phase, early, late]
    place = {}
    for i in range(groups):
        place[i] = (0, i)
        for j, m in enumerate(bases[1:]):
            place[m + i] = (1, j * groups + i)
        for j, m in enumerate(bases):
            place[(m ^ groups) + i] = (2, j * groups + i)
    part = structure(
        [block[m] for m in near], [place[m] for m in near], phase[:2], None, members, atoms, False
    )
    far_places = [(0, place[m][1]) for m in far_at]
    amps = structure([far_blocks], far_places, [late], part, members, atoms, True)

    stages = []
    sums = lax.broadcasted_iota(jnp.int32, amps.shape, 0) < channels
    while (1 << len(stages)) < outer:
        if stages:
            both_sums = amps.astype(f32) + stages[-1].astype(f32)
            amps = jnp.where(sums, both_sums, amps.astype(f32)).astype(bf16)
        stages.append(swap(amps, ((2 << len(stages)) - 1) * members))
    other = stages[-1] if stages else jnp.zeros_like(amps)

    columns = filters.shape[1]
    outs = [[place[m] for m in single], [place[m ^ groups] for m in single]]
    outs += [[place[m ^ core]] for m in direct for core in (0, groups)]
    keep, send, *straight = call(
        functools.partial(
            ewald_body,
            1.0 / math.sqrt(total_atoms),
            1.0 / math.sqrt(wave_index.shape[0] * groups),
            outs,
            len(phase),
        ),
        tuple(
            shape((len(blocks) * atoms, channels), bf16 if i else f32)
            for i, blocks in enumerate(outs)
        ),
        amps,
        other,
        mix_pair,
        filters,
        *phase,
        flops=2 * channels * columns * (2 * channels + members * atoms),
    )
    came = swap(send, groups)
    far_masks = [m ^ core for m in direct for core in (0, groups)]
    peers = [swap(x, m) for x, m in zip(straight, far_masks)]
    terms = keep + came.astype(f32)
    peers.append(terms[:atoms])
    for i, m in enumerate(single[1:], 1):
        peers.append(swap(terms[i * atoms : (i + 1) * atoms].astype(bf16), m))

    slots = neighbours.shape[1]
    steps = [(2 << i) - 1 for i in range(members.bit_length() - 1)]
    step_places = [(len(near), far_at[m]) if m in far_at else (near.index(m), 0) for m in steps]
    base = call(
        functools.partial(message_body, members, step_places, 1 + len(near)),
        (shape((atoms, channels), f32),),
        *[block[m] for m in near],
        far_blocks,
        *stages,
        msg_weight,
        chan_width.reshape(1, channels),
        pair_dist.T,
        neighbours.T,
        flops=3 * channels * atoms * slots * atoms,
        transcendentals=atoms * slots * channels,
    )
    return call(
        functools.partial(final_body, len(peers)),
        (shape((atoms, channels), bf16),),
        base,
        *peers,
        norm_gain.reshape(1, channels),
        in_weight,
        out_weight,
        flops=4 * atoms * channels * in_weight.shape[1],
    )


def layers(mesh):
    depths = {getattr(d, "coords", (0, 0, i))[2] for i, d in enumerate(mesh.devices[:, 0])}
    return len(depths)


def solution(mesh):
    placed = (
        P(both, None),
        P("space", None),
        P("kgrp", None),
        P("kgrp", None),
        P(),
        P(),
        P(),
        P(both, None),
        P(both, None),
        P(),
        P(),
        P(),
    )
    return jax.shard_map(
        functools.partial(local, layers(mesh)),
        mesh=mesh,
        in_specs=placed,
        out_specs=P(both, None),
        check_vma=False,
    )
```

```python
import functools
import math

import jax
import jax.numpy as jnp
import numpy as np
from jax import lax
from jax.experimental import pallas as pl
from jax.experimental.pallas import tpu as pltpu
from jax.sharding import PartitionSpec as P

box_side = 16.0
slab_step = 0.125
coord_rows = 16
bf16, f32 = jnp.bfloat16, jnp.float32

both = ("space", "kgrp")

vector_flops = 15000


def fit_cosine(degree):
    count = 64
    theta = (np.arange(count) + 0.5) * math.pi / count
    u = 0.125 * (1.0 + np.cos(theta))
    values = np.cos(2.0 * math.pi * np.sqrt(u))
    cheb = np.polynomial.chebyshev.Chebyshev.fit(u, values, degree, domain=[0.0, 0.25])
    return [float(c) for c in cheb.convert(kind=np.polynomial.Polynomial).coef]


cosine = fit_cosine(6)


def dot(a, b, dims):
    return lax.dot_general(a, b, (dims, ((), ())), preferred_element_type=f32)


def whole(count):
    return [pl.BlockSpec(memory_space=pltpu.VMEM)] * count


def call(body, outs, *args, flops=0, transcendentals=0):
    moved = sum(a.size * a.dtype.itemsize for a in (*args, *outs))
    return pl.pallas_call(
        body,
        out_shape=outs if len(outs) > 1 else outs[0],
        in_specs=whole(len(args)),
        out_specs=whole(len(outs)) if len(outs) > 1 else whole(1)[0],
        cost_estimate=pl.CostEstimate(
            flops=flops, bytes_accessed=moved, transcendentals=transcendentals
        ),
        compiler_params=pltpu.CompilerParams(vmem_limit_bytes=24 * 1024 * 1024),
    )(*args)


def shape(dims, dtype):
    return jax.ShapeDtypeStruct(dims, dtype)


def layer_member(members):
    member = lax.axis_index("space") * lax.axis_size("kgrp") + lax.axis_index("kgrp")
    return member & (members - 1)


def pack(features, positions, groups, slab_length):
    atoms, channels = features.shape
    scale = jnp.array([[1.0 / box_side], [1.0 / box_side], [1.0 / slab_length]], f32)
    turns = positions.T * scale
    high = lax.reduce_precision(turns, 8, 7)
    rest = turns - high
    middle = lax.reduce_precision(rest, 8, 7)
    parts = [high, middle, rest - middle, jnp.ones((1, groups * atoms), f32)]
    parts.append(jnp.zeros((coord_rows - 10, groups * atoms), f32))
    parts = jnp.concatenate(parts, axis=0).astype(bf16)
    split = [parts[:, i * atoms : (i + 1) * atoms] for i in range(groups)]
    return jnp.concatenate([features, *split], axis=0)


def fill_phases(block_ref, waves, groups, phase_ref):
    group = lax.axis_index("kgrp")
    atoms = phase_ref.shape[0] // groups
    for i in range(groups):
        row = pl.multiple_of(atoms + (group ^ i) * coord_rows, coord_rows)
        turns = dot(block_ref[pl.ds(row, coord_rows), :], waves, ((0,), (0,)))
        part = turns - jnp.round(turns)
        u = part * part
        value = jnp.full_like(u, cosine[-1])
        for c in cosine[-2::-1]:
            value = value * u + c
        phase_ref[i * atoms : (i + 1) * atoms, :] = value.astype(bf16)


def prepare_body(inner, groups, index_ref, block_ref, wave_ref, phase_ref):
    share = index_ref.shape[1] // inner
    own = lax.axis_index("space") & (inner - 1)
    counts = index_ref[...].astype(f32)
    halves = []
    for which in (own, own ^ 1):
        mine = counts[:, :share]
        for i in range(1, inner):
            mine = jnp.where(which == i, counts[:, i * share : (i + 1) * share], mine)
        halves += [mine, mine]
    counts = jnp.concatenate(halves, axis=1)
    column = lax.broadcasted_iota(jnp.int32, (1, 4 * share), 1)
    cosines = (column < share) | ((column >= 2 * share) & (column < 3 * share))
    quarter = jnp.where(cosines, 0.0, -0.25)
    zeros = jnp.zeros((coord_rows - 10, 4 * share), f32)
    waves = jnp.concatenate([counts, counts, counts, quarter, zeros], axis=0)
    wave_ref[...] = waves.astype(bf16)
    fill_phases(block_ref, wave_ref[...], groups, phase_ref)


def phase_body(groups, block_ref, wave_ref, phase_ref):
    fill_phases(block_ref, wave_ref[...], groups, phase_ref)


def add_blocks(block_refs, phase_ref, total):
    atoms = phase_ref.shape[0] // len(block_refs)
    for i, ref in enumerate(block_refs):
        phase = phase_ref[i * atoms : (i + 1) * atoms, :]
        term = dot(ref[:atoms, :], phase, ((0,), (0,)))
        total = term if total is None else total + term
    return total


def structure_body(*refs):
    *block_refs, phase_ref, sum_ref = refs
    sum_ref[...] = add_blocks(block_refs, phase_ref, None)


def stack(ref, total):
    channels = ref.shape[1]
    for i in range(total.shape[1] // channels):
        part = total[:, i * channels : (i + 1) * channels]
        ref[i * channels : (i + 1) * channels, :] = part.astype(ref.dtype)


def split_body(blocks, members, groups, masks, *refs):
    block_refs, refs = refs[:blocks], refs[blocks:]
    phase_ref, carry_ref, *far_refs, keep_ref, send_ref = refs
    total = add_blocks(block_refs, phase_ref, carry_ref[...])
    columns = total.shape[1] // 2
    stack(keep_ref, total[:, :columns])
    stack(send_ref, total[:, columns:])
    atoms = phase_ref.shape[0] // blocks
    halo = atoms // 4
    other = layer_member(members) ^ groups
    even = (other & 1) == 0
    edge = None
    for mask, ref in zip(masks, far_refs):
        rows = jnp.where(even, ref[atoms - halo : atoms, :], ref[:halo, :])
        if edge is None:
            edge = rows
        else:
            edge = jnp.where(reaches(other, even, mask), rows, edge)
    sums = send_ref.shape[0] - halo
    keep_ref[sums:, :] = jnp.zeros_like(keep_ref[sums:, :])
    send_ref[sums:, :] = edge


def reaches(member, even, mask):
    start = jnp.where(even, member, member + 1)
    return (start & mask) == (mask + 1) // 2


def mix_body(scale, a_ref, b_ref, mix_ref, filter_ref, y_ref):
    channels, columns = y_ref.shape
    tiles = [
        a_ref[i : i + channels, :].astype(f32) + b_ref[i : i + channels, :].astype(f32)
        for i in range(0, columns, channels)
    ]
    amps = (jnp.concatenate(tiles, axis=1) * scale).astype(bf16)
    half = amps.shape[1] // 2
    straight = dot(mix_ref[0], amps, ((0,), (0,)))
    crossed = dot(mix_ref[1], amps, ((0,), (0,)))
    crossed = jnp.concatenate([-crossed[:, half:], crossed[:, :half]], axis=1)
    y_ref[...] = (filter_ref[...] * (straight + crossed)).astype(bf16)


def near_body(phases, *refs):
    phase_refs, (y_ref, out_ref) = refs[:phases], refs[phases:]
    row = 0
    for ref in phase_refs:
        rows = ref.shape[0]
        out_ref[row : row + rows, :] = dot(ref[:, : y_ref.shape[1]], y_ref[...], ((1,), (1,)))
        row += rows


def far_body(phases, inv_scale, *refs):
    phase_refs, (y_ref, near_ref, *out_refs) = refs[:phases], refs[phases:]
    row = 0
    atoms = out_refs[0].shape[0]
    for ref in phase_refs:
        term = dot(ref[:, y_ref.shape[1] :], y_ref[...], ((1,), (1,)))
        for i in range(ref.shape[0] // atoms):
            block = term[i * atoms : (i + 1) * atoms] + near_ref[row : row + atoms, :]
            out = out_refs[row // atoms]
            out[...] = (block * inv_scale).astype(out.dtype)
            row += atoms


def hold_body(count, *refs):
    for a, b in zip(refs[:count], refs[count + 1 :]):
        b[...] = a[...]


def message_body(members, groups, masks, stages, *refs):
    feat_ref, *refs = refs
    near_refs, refs = refs[: len(masks)], refs[len(masks) :]
    core_ref, *refs = refs
    stage_refs, refs = refs[:stages], refs[stages:]
    msg_ref, width_ref, dist_ref, nbr_ref, base_ref = refs
    atoms, channels = dist_ref.shape[1], feat_ref.shape[1]
    features = feat_ref[:atoms, :]
    halo = atoms // 4
    member = layer_member(members)
    even = (member & 1) == 0
    layer = lax.axis_index("space") // (members // groups)

    def edge_of(ref):
        return ref[ref.shape[0] - halo :, :]

    start = jnp.where(even, layer, layer + 1)
    across = None
    for i, ref in enumerate(stage_refs):
        edge = edge_of(ref)
        across = edge if i == 0 else jnp.where((start & ((1 << i) - 1)) == 0, edge, across)
    far = edge_of(core_ref)
    if stages:
        ends = (member == 0) | (member == members - 1)
        far = jnp.where(ends, across, far)
    for mask, ref in zip(masks[1:], near_refs[1:]):
        rows = jnp.where(even, ref[atoms - halo : atoms, :], ref[:halo, :])
        far = jnp.where(reaches(member, even, mask), rows, far)
    beside = near_refs[0]
    before = jnp.where(even, far, beside[atoms - halo : atoms, :])
    after = jnp.where(even, beside[:halo, :], far)
    extended = jnp.concatenate([before, features, after], axis=0)
    projected = dot(msg_ref[...], extended, ((0,), (1,))).astype(bf16)
    row = lax.broadcasted_iota(jnp.int32, (extended.shape[0], atoms), 0)
    inverse = -1.0 / jnp.broadcast_to(width_ref[...], (atoms, channels)).T
    message = jnp.zeros((channels, atoms), f32)
    for j in range(nbr_ref.shape[0]):
        chosen = jnp.where(row == nbr_ref[j : j + 1, :], 1.0, 0.0).astype(bf16)
        nearby = dot(projected, chosen, ((1,), (0,)))
        message = message + jnp.exp(dist_ref[j : j + 1, :] * inverse) * nearby
    base_ref[...] = features.astype(f32) + message.T


def final_body(peers, *refs):
    base_ref, *refs = refs
    peer_refs, (gain_ref, in_ref, out_ref, result_ref) = refs[:peers], refs[peers:]
    mixed = base_ref[...]
    for ref in peer_refs:
        mixed = mixed + ref[...].astype(f32)
    inverse = lax.rsqrt(jnp.mean(mixed * mixed, axis=1, keepdims=True) + 1e-06)
    normed = (mixed * inverse * gain_ref[...]).astype(bf16)
    hidden = dot(normed, in_ref[...], ((1,), (0,)))
    half = 0.5 * hidden
    hidden = (half + half * jnp.tanh(half)).astype(bf16)
    result_ref[...] = (mixed + dot(hidden, out_ref[...], ((1,), (0,)))).astype(bf16)


def local(
    outer,
    features,
    positions,
    wave_index,
    wave_filter,
    mix_pair,
    msg_weight,
    chan_width,
    pair_dist,
    neighbours,
    norm_gain,
    in_weight,
    out_weight,
):
    atoms, channels = features.shape
    groups, space = lax.axis_size("kgrp"), lax.axis_size("space")
    inner = space // outer
    members = inner * groups
    devices = space * groups
    total_atoms = atoms * devices
    slab_length = total_atoms * slab_step
    share = wave_index.shape[0] // inner
    columns = 2 * share
    own_rows = groups * atoms

    def swap(x, mask):
        return lax.ppermute(x, both, [(i, i ^ mask) for i in range(devices)])

    near = [m for m in range(members) if not m & groups]
    bases = [m for m in near if m % groups == 0]
    block = {0: features}
    packed = pack(features, positions, groups, slab_length)
    for m in sorted(near[1:], key=lambda m: -m.bit_count()):
        block[m] = swap(features if m % groups else packed, m)
    waves, own_phase = call(
        functools.partial(prepare_body, inner, groups),
        (shape((coord_rows, 2 * columns), bf16), shape((own_rows, 2 * columns), bf16)),
        wave_index.T,
        packed,
        flops=vector_flops * 2 * own_rows * columns,
    )
    phase = [own_phase]
    for m in bases[1:]:
        phase.append(
            call(
                functools.partial(phase_body, groups),
                (shape((own_rows, 2 * columns), bf16),),
                block[m],
                waves,
                flops=vector_flops * own_rows * columns,
            )
        )

    work = 4 * own_rows * columns * channels
    part = None
    for m, rows in zip(bases[:-1], phase[:-1]):
        here = call(
            structure_body,
            (shape((channels, 2 * columns), f32),),
            *[block[m + i] if m + i else packed for i in range(groups)],
            rows,
            flops=work,
        )
        part = here if part is None else part + here
    chain = [(2 << i) - 1 for i in range(members.bit_length() - 1)]
    far_masks = [m for m in reversed(chain) if m & groups]
    height = columns + atoms // 4
    keep, send = call(
        functools.partial(split_body, groups, members, groups, far_masks),
        (shape((height, channels), f32), shape((height, channels), bf16)),
        *[block[bases[-1] + i] for i in range(groups)],
        phase[-1],
        part,
        *[block[m ^ groups] for m in far_masks],
        flops=work,
    )
    arrived = swap(send, groups)
    amps = (keep + arrived.astype(f32)).astype(bf16)

    stages = []
    sums = lax.broadcasted_iota(jnp.int32, amps.shape, 0) < columns
    while (1 << len(stages)) < outer:
        if stages:
            both_sums = amps.astype(f32) + stages[-1].astype(f32)
            amps = jnp.where(sums, both_sums, amps.astype(f32)).astype(bf16)
        stages.append(swap(amps, ((2 << len(stages)) - 1) * members))
    other = stages[-1] if stages else jnp.zeros_like(amps)
    held = (
        msg_weight,
        chan_width.reshape(1, channels),
        pair_dist.T,
        neighbours.T,
        norm_gain.reshape(1, channels),
        in_weight,
        out_weight,
    )
    held = call(
        functools.partial(hold_body, len(held)),
        tuple(shape(x.shape, x.dtype) for x in held),
        *held,
        amps,
        flops=2 * 10**9,
    )
    other, held = lax.optimization_barrier((other, held))
    msg_weight, chan_width, pair_dist, neighbours, norm_gain, in_weight, out_weight = held

    first = (lax.axis_index("space") % inner) * share
    filters = lax.dynamic_slice_in_dim(wave_filter, first, share, 0).T
    filters = jnp.concatenate([filters, filters], axis=1)
    y = call(
        functools.partial(mix_body, 1.0 / math.sqrt(total_atoms)),
        (shape((channels, columns), bf16),),
        amps,
        other,
        mix_pair,
        filters,
        flops=4 * channels * channels * columns,
    )
    y_far = swap(y, groups)
    work = 2 * len(near) * atoms * channels * columns
    near_terms = call(
        functools.partial(near_body, len(phase)),
        (shape((len(near) * atoms, channels), f32),),
        *phase,
        y,
        flops=work,
    )
    terms = call(
        functools.partial(far_body, len(phase), 1.0 / math.sqrt(wave_index.shape[0] * groups)),
        tuple(shape((atoms, channels), bf16 if m else f32) for m in near),
        *phase,
        y_far,
        near_terms,
        flops=work,
    )
    peers = [terms[0]]
    for m in sorted(near[1:], key=lambda m: -m.bit_count()):
        peers.append(swap(terms[near.index(m)], m))

    near_masks = [m for m in chain if not m & groups]
    base = call(
        functools.partial(message_body, members, groups, near_masks, len(stages)),
        (shape((atoms, channels), f32),),
        packed,
        *[block[m] for m in near_masks],
        arrived,
        *stages,
        msg_weight,
        chan_width,
        pair_dist,
        neighbours,
        flops=3 * channels * atoms * neighbours.shape[0] * atoms,
        transcendentals=atoms * neighbours.shape[0] * channels,
    )
    return call(
        functools.partial(final_body, len(peers)),
        (shape((atoms, channels), bf16),),
        base,
        *peers,
        norm_gain,
        in_weight,
        out_weight,
        flops=4 * atoms * channels * in_weight.shape[1],
    )


def layers(mesh):
    depths = {getattr(d, "coords", (0, 0, i))[2] for i, d in enumerate(mesh.devices[:, 0])}
    return len(depths)


def solution(mesh):
    placed = (
        P(both, None),
        P("space", None),
        P("kgrp", None),
        P("kgrp", None),
        P(),
        P(),
        P(),
        P(both, None),
        P(both, None),
        P(),
        P(),
        P(),
    )
    return jax.shard_map(
        functools.partial(local, layers(mesh)),
        mesh=mesh,
        in_specs=placed,
        out_specs=P(both, None),
        check_vma=False,
    )
```

```python
import functools
import math

import jax
import jax.numpy as jnp
import numpy as np
from jax import lax
from jax.experimental import pallas as pl
from jax.experimental.pallas import tpu as pltpu
from jax.sharding import PartitionSpec as P

box_side = 16.0
slab_step = 0.125
coord_rows = 16
bf16, f32 = jnp.bfloat16, jnp.float32

both = ("space", "kgrp")

vector_flops = 15000


def fit_cosine(degree):
    count = 64
    theta = (np.arange(count) + 0.5) * math.pi / count
    u = 0.125 * (1.0 + np.cos(theta))
    values = np.cos(2.0 * math.pi * np.sqrt(u))
    cheb = np.polynomial.chebyshev.Chebyshev.fit(u, values, degree, domain=[0.0, 0.25])
    return [float(c) for c in cheb.convert(kind=np.polynomial.Polynomial).coef]


cosine = fit_cosine(6)


def dot(a, b, dims):
    return lax.dot_general(a, b, (dims, ((), ())), preferred_element_type=f32)


def whole(count):
    return [pl.BlockSpec(memory_space=pltpu.VMEM)] * count


def call(body, outs, *args, flops=0, transcendentals=0):
    moved = sum(a.size * a.dtype.itemsize for a in (*args, *outs))
    return pl.pallas_call(
        body,
        out_shape=outs if len(outs) > 1 else outs[0],
        in_specs=whole(len(args)),
        out_specs=whole(len(outs)) if len(outs) > 1 else whole(1)[0],
        cost_estimate=pl.CostEstimate(
            flops=flops, bytes_accessed=moved, transcendentals=transcendentals
        ),
        compiler_params=pltpu.CompilerParams(vmem_limit_bytes=24 * 1024 * 1024),
    )(*args)


def shape(dims, dtype):
    return jax.ShapeDtypeStruct(dims, dtype)


def wave_share(inner):
    space = lax.axis_index("space")
    return (space ^ (space // inner & 1)) & (inner - 1)


def layer_member(members):
    member = lax.axis_index("space") * lax.axis_size("kgrp") + lax.axis_index("kgrp")
    return member & (members - 1)


def pack(features, positions, groups, slab_length):
    atoms, channels = features.shape
    scale = jnp.array([[1.0 / box_side], [1.0 / box_side], [1.0 / slab_length]], f32)
    turns = positions.T * scale
    high = lax.reduce_precision(turns, 8, 7)
    rest = turns - high
    middle = lax.reduce_precision(rest, 8, 7)
    parts = [high, middle, rest - middle, jnp.ones((1, groups * atoms), f32)]
    parts.append(jnp.zeros((coord_rows - 10, groups * atoms), f32))
    parts = jnp.concatenate(parts, axis=0).astype(bf16)
    split = [parts[:, i * atoms : (i + 1) * atoms] for i in range(groups)]
    return jnp.concatenate([features, *split], axis=0)


def fill_phases(block_ref, waves, groups, phase_ref):
    group = lax.axis_index("kgrp")
    atoms = phase_ref.shape[0] // groups
    for i in range(groups):
        row = pl.multiple_of(atoms + (group ^ i) * coord_rows, coord_rows)
        turns = dot(block_ref[pl.ds(row, coord_rows), :], waves, ((0,), (0,)))
        part = turns - jnp.round(turns)
        u = part * part
        value = jnp.full_like(u, cosine[-1])
        for c in cosine[-2::-1]:
            value = value * u + c
        phase_ref[i * atoms : (i + 1) * atoms, :] = value.astype(bf16)


def prepare_body(inner, groups, index_ref, block_ref, wave_ref, phase_ref):
    share = index_ref.shape[1] // inner
    own = wave_share(inner)
    counts = index_ref[...].astype(f32)
    halves = []
    for which in (own, own ^ 1):
        mine = counts[:, :share]
        for i in range(1, inner):
            mine = jnp.where(which == i, counts[:, i * share : (i + 1) * share], mine)
        halves += [mine, mine]
    counts = jnp.concatenate(halves, axis=1)
    column = lax.broadcasted_iota(jnp.int32, (1, 4 * share), 1)
    cosines = (column < share) | ((column >= 2 * share) & (column < 3 * share))
    quarter = jnp.where(cosines, 0.0, -0.25)
    zeros = jnp.zeros((coord_rows - 10, 4 * share), f32)
    waves = jnp.concatenate([counts, counts, counts, quarter, zeros], axis=0)
    wave_ref[...] = waves.astype(bf16)
    fill_phases(block_ref, wave_ref[...], groups, phase_ref)


def phase_body(groups, block_ref, wave_ref, phase_ref):
    fill_phases(block_ref, wave_ref[...], groups, phase_ref)


def features_body(block_ref, out_ref):
    out_ref[...] = block_ref[: out_ref.shape[0], :]


def add_blocks(block_refs, phase_ref, total):
    atoms = phase_ref.shape[0] // len(block_refs)
    for i, ref in enumerate(block_refs):
        phase = phase_ref[i * atoms : (i + 1) * atoms, :]
        term = dot(ref[:atoms, :], phase, ((0,), (0,)))
        total = term if total is None else total + term
    return total


def structure_body(*refs):
    *block_refs, phase_ref, sum_ref = refs
    sum_ref[...] = add_blocks(block_refs, phase_ref, None)


def stack(ref, total):
    channels = ref.shape[1]
    for i in range(total.shape[1] // channels):
        part = total[:, i * channels : (i + 1) * channels]
        ref[i * channels : (i + 1) * channels, :] = part.astype(ref.dtype)


def split_body(blocks, members, groups, masks, *refs):
    block_refs, refs = refs[:blocks], refs[blocks:]
    phase_ref, carry_ref, *far_refs, end_ref, keep_ref, send_ref = refs
    total = add_blocks(block_refs, phase_ref, carry_ref[...])
    columns = total.shape[1] // 2
    stack(keep_ref, total[:, :columns])
    stack(send_ref, total[:, columns:])
    atoms = phase_ref.shape[0] // blocks
    halo = atoms // 4
    sums = keep_ref.shape[0] - halo
    other = layer_member(members) ^ groups
    even = (other & 1) == 0

    def beside(ref):
        return jnp.where(even, ref[atoms - halo : atoms, :], ref[:halo, :])

    keep_ref[sums:, :] = jnp.zeros_like(keep_ref[sums:, :])
    send_ref[sums : sums + halo, :] = beside(end_ref)
    needed = beside(far_refs[0])
    for mask, ref in zip(masks[1:], far_refs[1:]):
        needed = jnp.where(reaches(other, even, mask), beside(ref), needed)
    send_ref[sums + halo :, :] = needed


def reaches(member, even, mask):
    start = jnp.where(even, member, member + 1)
    return (start & mask) == (mask + 1) // 2


def mix_body(scale, a_ref, b_ref, mix_ref, filter_ref, y_ref):
    channels, columns = y_ref.shape
    tiles = [
        a_ref[i : i + channels, :].astype(f32) + b_ref[i : i + channels, :].astype(f32)
        for i in range(0, columns, channels)
    ]
    amps = (jnp.concatenate(tiles, axis=1) * scale).astype(bf16)
    half = amps.shape[1] // 2
    straight = dot(mix_ref[0], amps, ((0,), (0,)))
    crossed = dot(mix_ref[1], amps, ((0,), (0,)))
    crossed = jnp.concatenate([-crossed[:, half:], crossed[:, :half]], axis=1)
    y_ref[...] = (filter_ref[...] * (straight + crossed)).astype(bf16)


def near_body(phases, *refs):
    phase_refs, (y_ref, out_ref) = refs[:phases], refs[phases:]
    row = 0
    for ref in phase_refs:
        rows = ref.shape[0]
        out_ref[row : row + rows, :] = dot(ref[:, : y_ref.shape[1]], y_ref[...], ((1,), (1,)))
        row += rows


def far_body(phases, inv_scale, *refs):
    phase_refs, (y_ref, near_ref, *out_refs) = refs[:phases], refs[phases:]
    row = 0
    atoms = out_refs[0].shape[0]
    for ref in phase_refs:
        term = dot(ref[:, y_ref.shape[1] :], y_ref[...], ((1,), (1,)))
        for i in range(ref.shape[0] // atoms):
            block = term[i * atoms : (i + 1) * atoms] + near_ref[row : row + atoms, :]
            out = out_refs[row // atoms]
            out[...] = (block * inv_scale).astype(out.dtype)
            row += atoms


def hold_body(count, *refs):
    for a, b in zip(refs[:count], refs[count + 1 :]):
        b[...] = a[...]


def message_body(members, groups, masks, stages, *refs):
    feat_ref, *refs = refs
    near_refs, refs = refs[: len(masks)], refs[len(masks) :]
    core_ref, *refs = refs
    stage_refs, refs = refs[:stages], refs[stages:]
    msg_ref, width_ref, dist_ref, nbr_ref, base_ref = refs
    atoms, channels = dist_ref.shape[1], feat_ref.shape[1]
    features = feat_ref[:atoms, :]
    halo = atoms // 4
    member = layer_member(members)
    even = (member & 1) == 0
    layer = lax.axis_index("space") // (members // groups)

    def edge_of(ref):
        return ref[ref.shape[0] - halo :, :]

    start = jnp.where(even, layer, layer + 1)
    across = None
    for i, ref in enumerate(stage_refs):
        edge = edge_of(ref)
        across = edge if i == 0 else jnp.where((start & ((1 << i) - 1)) == 0, edge, across)
    far = edge_of(core_ref)
    if stages:
        ends = (member == 0) | (member == members - 1)
        far = jnp.where(ends, across, far)
    for mask, ref in zip(masks[1:], near_refs[1:]):
        rows = jnp.where(even, ref[atoms - halo : atoms, :], ref[:halo, :])
        far = jnp.where(reaches(member, even, mask), rows, far)
    beside = near_refs[0]
    before = jnp.where(even, far, beside[atoms - halo : atoms, :])
    after = jnp.where(even, beside[:halo, :], far)
    extended = jnp.concatenate([before, features, after], axis=0)
    projected = dot(msg_ref[...], extended, ((0,), (1,))).astype(bf16)
    row = lax.broadcasted_iota(jnp.int32, (extended.shape[0], atoms), 0)
    inverse = -1.0 / jnp.broadcast_to(width_ref[...], (atoms, channels)).T
    message = jnp.zeros((channels, atoms), f32)
    for j in range(nbr_ref.shape[0]):
        chosen = jnp.where(row == nbr_ref[j : j + 1, :], 1.0, 0.0).astype(bf16)
        nearby = dot(projected, chosen, ((1,), (0,)))
        message = message + jnp.exp(dist_ref[j : j + 1, :] * inverse) * nearby
    base_ref[...] = features.astype(f32) + message.T


def final_body(peers, *refs):
    base_ref, *refs = refs
    peer_refs, (gain_ref, in_ref, out_ref, result_ref) = refs[:peers], refs[peers:]
    mixed = base_ref[...]
    for ref in peer_refs:
        mixed = mixed + ref[...].astype(f32)
    inverse = lax.rsqrt(jnp.mean(mixed * mixed, axis=1, keepdims=True) + 1e-06)
    normed = (mixed * inverse * gain_ref[...]).astype(bf16)
    hidden = dot(normed, in_ref[...], ((1,), (0,)))
    half = 0.5 * hidden
    hidden = (half + half * jnp.tanh(half)).astype(bf16)
    result_ref[...] = (mixed + dot(hidden, out_ref[...], ((1,), (0,)))).astype(bf16)


def local(
    outer,
    features,
    positions,
    wave_index,
    wave_filter,
    mix_pair,
    msg_weight,
    chan_width,
    pair_dist,
    neighbours,
    norm_gain,
    in_weight,
    out_weight,
):
    atoms, channels = features.shape
    groups, space = lax.axis_size("kgrp"), lax.axis_size("space")
    inner = space // outer
    members = inner * groups
    devices = space * groups
    total_atoms = atoms * devices
    slab_length = total_atoms * slab_step
    share = wave_index.shape[0] // inner
    columns = 2 * share
    own_rows = groups * atoms

    def swap(x, mask):
        return lax.ppermute(x, both, [(i, i ^ mask) for i in range(devices)])

    bases = []
    for i in range(inner // 2):
        bases.append((2 * i + i.bit_count() % 2) * groups)
    near = [m + i for m in bases for i in range(groups)]
    farthest = sorted(near[1:], key=lambda m: -(m & ~groups).bit_count())
    block = {0: features}
    packed = pack(features, positions, groups, slab_length)
    copied = call(
        features_body, (shape((atoms, channels), bf16),), packed, flops=vector_flops * 300000
    )
    for m in near[1:]:
        source = packed if m % groups == 0 else features if m < groups else copied
        block[m] = swap(source, m)
    waves, own_phase = call(
        functools.partial(prepare_body, inner, groups),
        (shape((coord_rows, 2 * columns), bf16), shape((own_rows, 2 * columns), bf16)),
        wave_index.T,
        packed,
        flops=vector_flops * 2 * own_rows * columns,
    )
    phase = [own_phase]
    for m in bases[1:]:
        phase.append(
            call(
                functools.partial(phase_body, groups),
                (shape((own_rows, 2 * columns), bf16),),
                block[m],
                waves,
                flops=vector_flops * own_rows * columns,
            )
        )

    work = 4 * own_rows * columns * channels
    part = None
    for m, rows in zip(bases[:-1], phase[:-1]):
        here = call(
            structure_body,
            (shape((channels, 2 * columns), f32),),
            *[block[m + i] if m + i else packed for i in range(groups)],
            rows,
            flops=work,
        )
        part = here if part is None else part + here
    chain = [(2 << i) - 1 for i in range(members.bit_length() - 1)]
    far_masks = [m for m in reversed(chain) if m not in near]
    height = columns + atoms // 4
    keep, send = call(
        functools.partial(split_body, groups, members, groups, far_masks),
        (shape((height, channels), f32), shape((height + atoms // 4, channels), bf16)),
        *[block[bases[-1] + i] for i in range(groups)],
        phase[-1],
        part,
        *[block[m ^ groups] for m in far_masks],
        block[members - 1],
        flops=work,
    )
    arrived = swap(send, groups)
    amps = (keep + arrived[:height].astype(f32)).astype(bf16)

    stages = []
    sums = lax.broadcasted_iota(jnp.int32, amps.shape, 0) < columns
    while (1 << len(stages)) < outer:
        if stages:
            both_sums = amps.astype(f32) + stages[-1].astype(f32)
            amps = jnp.where(sums, both_sums, amps.astype(f32)).astype(bf16)
        stages.append(swap(amps, ((2 << len(stages)) - 1) * members ^ groups))
    other = stages[-1] if stages else jnp.zeros_like(amps)
    held = (
        msg_weight,
        chan_width.reshape(1, channels),
        pair_dist.T,
        neighbours.T,
        norm_gain.reshape(1, channels),
        in_weight,
        out_weight,
    )
    held = call(
        functools.partial(hold_body, len(held)),
        tuple(shape(x.shape, x.dtype) for x in held),
        *held,
        amps,
        flops=2 * 10**9,
    )
    other, held = lax.optimization_barrier((other, held))
    msg_weight, chan_width, pair_dist, neighbours, norm_gain, in_weight, out_weight = held

    first = wave_share(inner) * share
    filters = lax.dynamic_slice_in_dim(wave_filter, first, share, 0).T
    filters = jnp.concatenate([filters, filters], axis=1)
    y = call(
        functools.partial(mix_body, 1.0 / math.sqrt(total_atoms)),
        (shape((channels, columns), bf16),),
        amps,
        other,
        mix_pair,
        filters,
        flops=4 * channels * channels * columns,
    )
    y_far = swap(y, groups)
    work = 2 * len(near) * atoms * channels * columns
    near_terms = call(
        functools.partial(near_body, len(phase)),
        (shape((len(near) * atoms, channels), f32),),
        *phase,
        y,
        flops=work,
    )
    terms = call(
        functools.partial(far_body, len(phase), 1.0 / math.sqrt(wave_index.shape[0] * groups)),
        tuple(shape((atoms, channels), bf16 if m else f32) for m in near),
        *phase,
        y_far,
        near_terms,
        flops=work,
    )
    peers = [terms[0]]
    for m in farthest:
        peers.append(swap(terms[near.index(m)], m))

    near_masks = [m for m in chain if m in near]
    base = call(
        functools.partial(message_body, members, groups, near_masks, len(stages)),
        (shape((atoms, channels), f32),),
        packed,
        *[block[m] for m in near_masks],
        arrived,
        *stages,
        msg_weight,
        chan_width,
        pair_dist,
        neighbours,
        flops=3 * channels * atoms * neighbours.shape[0] * atoms,
        transcendentals=atoms * neighbours.shape[0] * channels,
    )
    return call(
        functools.partial(final_body, len(peers)),
        (shape((atoms, channels), bf16),),
        base,
        *peers,
        norm_gain,
        in_weight,
        out_weight,
        flops=4 * atoms * channels * in_weight.shape[1],
    )


def layers(mesh):
    depths = {getattr(d, "coords", (0, 0, i))[2] for i, d in enumerate(mesh.devices[:, 0])}
    return len(depths)


def solution(mesh):
    placed = (
        P(both, None),
        P("space", None),
        P("kgrp", None),
        P("kgrp", None),
        P(),
        P(),
        P(),
        P(both, None),
        P(both, None),
        P(),
        P(),
        P(),
    )
    return jax.shard_map(
        functools.partial(local, layers(mesh)),
        mesh=mesh,
        in_specs=placed,
        out_specs=P(both, None),
        check_vma=False,
    )
```

```python
import functools
import math

import jax
import jax.numpy as jnp
import numpy as np
from jax import lax
from jax.experimental import pallas as pl
from jax.experimental.pallas import tpu as pltpu
from jax.sharding import PartitionSpec as P

box_side = 16.0
slab_step = 0.125
coord_rows = 16
bf16, f32 = jnp.bfloat16, jnp.float32

both = ("space", "kgrp")

vector_flops = 15000


def fit_cosine(degree):
    count = 64
    theta = (np.arange(count) + 0.5) * math.pi / count
    u = 0.125 * (1.0 + np.cos(theta))
    values = np.cos(2.0 * math.pi * np.sqrt(u))
    cheb = np.polynomial.chebyshev.Chebyshev.fit(u, values, degree, domain=[0.0, 0.25])
    return [float(c) for c in cheb.convert(kind=np.polynomial.Polynomial).coef]


cosine = fit_cosine(6)


def dot(a, b, dims):
    return lax.dot_general(a, b, (dims, ((), ())), preferred_element_type=f32)


def whole(count):
    return [pl.BlockSpec(memory_space=pltpu.VMEM)] * count


def call(body, outs, *args, flops=0, transcendentals=0):
    moved = sum(a.size * a.dtype.itemsize for a in (*args, *outs))
    return pl.pallas_call(
        body,
        out_shape=outs if len(outs) > 1 else outs[0],
        in_specs=whole(len(args)),
        out_specs=whole(len(outs)) if len(outs) > 1 else whole(1)[0],
        cost_estimate=pl.CostEstimate(
            flops=flops, bytes_accessed=moved, transcendentals=transcendentals
        ),
        compiler_params=pltpu.CompilerParams(vmem_limit_bytes=24 * 1024 * 1024),
    )(*args)


def shape(dims, dtype):
    return jax.ShapeDtypeStruct(dims, dtype)


def wave_share(inner):
    space = lax.axis_index("space")
    return (space ^ (space // inner & 1)) & (inner - 1)


def layer_member(members):
    member = lax.axis_index("space") * lax.axis_size("kgrp") + lax.axis_index("kgrp")
    return member & (members - 1)


def pack(features, positions, groups, slab_length):
    atoms, channels = features.shape
    row = lax.broadcasted_iota(jnp.int32, (coord_rows, atoms), 0)
    scale = jnp.where(row % 3 == 2, 1.0 / slab_length, 1.0 / box_side)
    rows = [features]
    for i in range(groups):
        own = positions[i * atoms : (i + 1) * atoms].T
        turns = jnp.pad(jnp.concatenate([own, own, own], axis=0), ((0, coord_rows - 9), (0, 0))) * scale
        high = lax.reduce_precision(turns, 8, 7)
        rest = turns - high
        middle = lax.reduce_precision(rest, 8, 7)
        parts = jnp.where(row < 3, high, jnp.where(row < 6, middle, rest - middle))
        parts = jnp.where(row < 9, parts, jnp.where(row == 9, 1.0, 0.0))
        rows.append(parts.astype(bf16))
    return jnp.concatenate(rows, axis=0)


def fill_phases(block_ref, waves, groups, phase_ref):
    group = lax.axis_index("kgrp")
    atoms = phase_ref.shape[0] // groups
    for i in range(groups):
        row = pl.multiple_of(atoms + (group ^ i) * coord_rows, coord_rows)
        turns = dot(block_ref[pl.ds(row, coord_rows), :], waves, ((0,), (0,)))
        part = turns - jnp.round(turns)
        u = part * part
        value = jnp.full_like(u, cosine[-1])
        for c in cosine[-2::-1]:
            value = value * u + c
        phase_ref[i * atoms : (i + 1) * atoms, :] = value.astype(bf16)


def prepare_body(inner, groups, index_ref, block_ref, wave_ref, phase_ref):
    share = index_ref.shape[1] // inner
    own = wave_share(inner)
    counts = index_ref[...].astype(f32)
    halves = []
    for which in (own, own ^ 1):
        mine = counts[:, :share]
        for i in range(1, inner):
            mine = jnp.where(which == i, counts[:, i * share : (i + 1) * share], mine)
        halves += [mine, mine]
    counts = jnp.concatenate(halves, axis=1)
    column = lax.broadcasted_iota(jnp.int32, (1, 4 * share), 1)
    cosines = (column < share) | ((column >= 2 * share) & (column < 3 * share))
    quarter = jnp.where(cosines, 0.0, -0.25)
    zeros = jnp.zeros((coord_rows - 10, 4 * share), f32)
    waves = jnp.concatenate([counts, counts, counts, quarter, zeros], axis=0)
    wave_ref[...] = waves.astype(bf16)
    fill_phases(block_ref, wave_ref[...], groups, phase_ref)


def phase_body(groups, block_ref, wave_ref, phase_ref):
    fill_phases(block_ref, wave_ref[...], groups, phase_ref)


def features_body(block_ref, out_ref):
    out_ref[...] = block_ref[: out_ref.shape[0], :]


def add_blocks(block_refs, phase_ref, total):
    atoms = phase_ref.shape[0] // len(block_refs)
    for i, ref in enumerate(block_refs):
        phase = phase_ref[i * atoms : (i + 1) * atoms, :]
        term = dot(ref[:atoms, :], phase, ((0,), (0,)))
        total = term if total is None else total + term
    return total


def structure_body(*refs):
    *block_refs, phase_ref, sum_ref = refs
    sum_ref[...] = add_blocks(block_refs, phase_ref, None)


def stack(ref, total):
    channels = ref.shape[1]
    for i in range(total.shape[1] // channels):
        part = total[:, i * channels : (i + 1) * channels]
        ref[i * channels : (i + 1) * channels, :] = part.astype(ref.dtype)


def split_body(blocks, members, groups, masks, *refs):
    block_refs, refs = refs[:blocks], refs[blocks:]
    phase_ref, carry_ref, *far_refs, end_ref, keep_ref, send_ref = refs
    total = add_blocks(block_refs, phase_ref, carry_ref[...])
    columns = total.shape[1] // 2
    stack(keep_ref, total[:, :columns])
    stack(send_ref, total[:, columns:])
    atoms = phase_ref.shape[0] // blocks
    halo = atoms // 4
    sums = keep_ref.shape[0] - halo
    other = layer_member(members) ^ groups
    even = (other & 1) == 0

    def beside(ref):
        return jnp.where(even, ref[atoms - halo : atoms, :], ref[:halo, :])

    keep_ref[sums:, :] = jnp.zeros_like(keep_ref[sums:, :])
    send_ref[sums : sums + halo, :] = beside(end_ref)
    needed = beside(far_refs[0])
    for mask, ref in zip(masks[1:], far_refs[1:]):
        needed = jnp.where(reaches(other, even, mask), beside(ref), needed)
    send_ref[sums + halo :, :] = needed


def reaches(member, even, mask):
    start = jnp.where(even, member, member + 1)
    return (start & mask) == (mask + 1) // 2


def mix_body(scale, a_ref, b_ref, mix_ref, filter_ref, y_ref):
    channels, columns = y_ref.shape
    tiles = [
        a_ref[i : i + channels, :].astype(f32) + b_ref[i : i + channels, :].astype(f32)
        for i in range(0, columns, channels)
    ]
    amps = (jnp.concatenate(tiles, axis=1) * scale).astype(bf16)
    half = amps.shape[1] // 2
    straight = dot(mix_ref[0], amps, ((0,), (0,)))
    crossed = dot(mix_ref[1], amps, ((0,), (0,)))
    crossed = jnp.concatenate([-crossed[:, half:], crossed[:, :half]], axis=1)
    y_ref[...] = (filter_ref[...] * (straight + crossed)).astype(bf16)


def near_body(phases, *refs):
    phase_refs, (y_ref, out_ref) = refs[:phases], refs[phases:]
    row = 0
    for ref in phase_refs:
        rows = ref.shape[0]
        out_ref[row : row + rows, :] = dot(ref[:, : y_ref.shape[1]], y_ref[...], ((1,), (1,)))
        row += rows


def far_body(phases, inv_scale, *refs):
    phase_refs, (y_ref, near_ref, *out_refs) = refs[:phases], refs[phases:]
    row = 0
    atoms = out_refs[0].shape[0]
    for ref in phase_refs:
        term = dot(ref[:, y_ref.shape[1] :], y_ref[...], ((1,), (1,)))
        for i in range(ref.shape[0] // atoms):
            block = term[i * atoms : (i + 1) * atoms] + near_ref[row : row + atoms, :]
            out = out_refs[row // atoms]
            out[...] = (block * inv_scale).astype(out.dtype)
            row += atoms


def hold_body(count, *refs):
    for a, b in zip(refs[:count], refs[count + 1 :]):
        b[...] = a[...]


def message_body(members, groups, masks, stages, *refs):
    feat_ref, *refs = refs
    near_refs, refs = refs[: len(masks)], refs[len(masks) :]
    core_ref, *refs = refs
    stage_refs, refs = refs[:stages], refs[stages:]
    msg_ref, width_ref, dist_ref, nbr_ref, base_ref = refs
    atoms, channels = dist_ref.shape[1], feat_ref.shape[1]
    features = feat_ref[:atoms, :]
    halo = atoms // 4
    member = layer_member(members)
    even = (member & 1) == 0
    layer = lax.axis_index("space") // (members // groups)

    def edge_of(ref):
        return ref[ref.shape[0] - halo :, :]

    start = jnp.where(even, layer, layer + 1)
    across = None
    for i, ref in enumerate(stage_refs):
        edge = edge_of(ref)
        across = edge if i == 0 else jnp.where((start & ((1 << i) - 1)) == 0, edge, across)
    far = edge_of(core_ref)
    ends = (member == 0) | (member == members - 1)
    if not stages:
        across = jnp.where(even, near_refs[-1][atoms - halo : atoms, :], near_refs[-1][:halo, :])
    far = jnp.where(ends, across, far)
    for mask, ref in zip(masks[1:], near_refs[1:]):
        rows = jnp.where(even, ref[atoms - halo : atoms, :], ref[:halo, :])
        far = jnp.where(reaches(member, even, mask), rows, far)
    beside = near_refs[0]
    before = jnp.where(even, far, beside[atoms - halo : atoms, :])
    after = jnp.where(even, beside[:halo, :], far)
    extended = jnp.concatenate([before, features, after], axis=0)
    projected = dot(msg_ref[...], extended, ((0,), (1,))).astype(bf16)
    row = lax.broadcasted_iota(jnp.int32, (extended.shape[0], atoms), 0)
    inverse = -1.0 / jnp.broadcast_to(width_ref[...], (atoms, channels)).T
    message = jnp.zeros((channels, atoms), f32)
    for j in range(nbr_ref.shape[0]):
        chosen = jnp.where(row == nbr_ref[j : j + 1, :], 1.0, 0.0).astype(bf16)
        nearby = dot(projected, chosen, ((1,), (0,)))
        message = message + jnp.exp(dist_ref[j : j + 1, :] * inverse) * nearby
    base_ref[...] = features.astype(f32) + message.T


def final_body(peers, *refs):
    base_ref, *refs = refs
    peer_refs, (gain_ref, in_ref, out_ref, result_ref) = refs[:peers], refs[peers:]
    mixed = base_ref[...]
    for ref in peer_refs:
        mixed = mixed + ref[...].astype(f32)
    inverse = lax.rsqrt(jnp.mean(mixed * mixed, axis=1, keepdims=True) + 1e-06)
    normed = (mixed * inverse * gain_ref[...]).astype(bf16)
    hidden = dot(normed, in_ref[...], ((1,), (0,)))
    half = 0.5 * hidden
    hidden = (half + half * jnp.tanh(half)).astype(bf16)
    result_ref[...] = (mixed + dot(hidden, out_ref[...], ((1,), (0,)))).astype(bf16)


def local(
    outer,
    features,
    positions,
    wave_index,
    wave_filter,
    mix_pair,
    msg_weight,
    chan_width,
    pair_dist,
    neighbours,
    norm_gain,
    in_weight,
    out_weight,
):
    atoms, channels = features.shape
    groups, space = lax.axis_size("kgrp"), lax.axis_size("space")
    inner = space // outer
    members = inner * groups
    devices = space * groups
    total_atoms = atoms * devices
    slab_length = total_atoms * slab_step
    share = wave_index.shape[0] // inner
    columns = 2 * share
    own_rows = groups * atoms

    def swap(x, mask):
        return lax.ppermute(x, both, [(i, i ^ mask) for i in range(devices)])

    bases = []
    for i in range(inner // 2):
        bases.append((2 * i + i.bit_count() % 2) * groups)
    near = [m + i for m in bases for i in range(groups)]
    block = {0: features}
    packed = pack(features, positions, groups, slab_length)
    source = packed
    for m in sorted(near[1:], key=lambda m: (m % groups != 0, m > groups)):
        block[m] = swap(source, m)
        source = call(
            features_body, (shape((atoms, channels), bf16),), source, flops=vector_flops * 300000
        )
    waves, own_phase = call(
        functools.partial(prepare_body, inner, groups),
        (shape((coord_rows, 2 * columns), bf16), shape((own_rows, 2 * columns), bf16)),
        wave_index.T,
        packed,
        flops=vector_flops * 2 * own_rows * columns,
    )
    phase = [own_phase]
    for m in bases[1:]:
        phase.append(
            call(
                functools.partial(phase_body, groups),
                (shape((own_rows, 2 * columns), bf16),),
                block[m],
                waves,
                flops=vector_flops * own_rows * columns,
            )
        )

    work = 4 * own_rows * columns * channels
    part = None
    for m, rows in zip(bases[:-1], phase[:-1]):
        here = call(
            structure_body,
            (shape((channels, 2 * columns), f32),),
            *[block[m + i] if m + i else packed for i in range(groups)],
            rows,
            flops=work,
        )
        part = here if part is None else part + here
    chain = [(2 << i) - 1 for i in range(members.bit_length() - 1)]
    far_masks = [m for m in reversed(chain) if m not in near]
    height = columns + atoms // 4
    keep, send = call(
        functools.partial(split_body, groups, members, groups, far_masks),
        (shape((height, channels), f32), shape((height + atoms // 4, channels), bf16)),
        *[block[bases[-1] + i] for i in range(groups)],
        phase[-1],
        part,
        *[block[m ^ groups] for m in far_masks],
        block[members - 1],
        flops=work,
    )
    arrived = swap(send, groups)
    amps = (keep + arrived[:height].astype(f32)).astype(bf16)

    stages = []
    sums = lax.broadcasted_iota(jnp.int32, amps.shape, 0) < columns
    while (1 << len(stages)) < outer:
        if stages:
            both_sums = amps.astype(f32) + stages[-1].astype(f32)
            amps = jnp.where(sums, both_sums, amps.astype(f32)).astype(bf16)
        stages.append(swap(amps, ((2 << len(stages)) - 1) * members ^ groups))
    other = stages[-1] if stages else jnp.zeros_like(amps)
    held = (
        msg_weight,
        chan_width.reshape(1, channels),
        pair_dist.T,
        neighbours.T,
        norm_gain.reshape(1, channels),
        in_weight,
        out_weight,
    )
    held = call(
        functools.partial(hold_body, len(held)),
        tuple(shape(x.shape, x.dtype) for x in held),
        *held,
        amps,
        flops=2 * 10**9,
    )
    other, held = lax.optimization_barrier((other, held))
    msg_weight, chan_width, pair_dist, neighbours, norm_gain, in_weight, out_weight = held

    first = wave_share(inner) * share
    filters = lax.dynamic_slice_in_dim(wave_filter, first, share, 0).T
    filters = jnp.concatenate([filters, filters], axis=1)
    y = call(
        functools.partial(mix_body, 1.0 / math.sqrt(total_atoms)),
        (shape((channels, columns), bf16),),
        amps,
        other,
        mix_pair,
        filters,
        flops=4 * channels * channels * columns,
    )
    y_far = swap(y, groups)
    work = 2 * len(near) * atoms * channels * columns
    near_terms = call(
        functools.partial(near_body, len(phase)),
        (shape((len(near) * atoms, channels), f32),),
        *phase,
        y,
        flops=work,
    )
    terms = call(
        functools.partial(far_body, len(phase), 1.0 / math.sqrt(wave_index.shape[0] * groups)),
        tuple(shape((atoms, channels), bf16 if m else f32) for m in near),
        *phase,
        y_far,
        near_terms,
        flops=work,
    )
    peers = [terms[0]]
    for m in sorted(near[1:], key=lambda m: -(m & ~groups).bit_count()):
        peers.append(swap(terms[near.index(m)], m))

    near_masks = [m for m in chain if m in near]
    base = call(
        functools.partial(message_body, members, groups, near_masks, len(stages)),
        (shape((atoms, channels), f32),),
        packed,
        *[block[m] for m in near_masks],
        arrived,
        *stages,
        msg_weight,
        chan_width,
        pair_dist,
        neighbours,
        flops=3 * channels * atoms * neighbours.shape[0] * atoms,
        transcendentals=atoms * neighbours.shape[0] * channels,
    )
    return call(
        functools.partial(final_body, len(peers)),
        (shape((atoms, channels), bf16),),
        base,
        *peers,
        norm_gain,
        in_weight,
        out_weight,
        flops=4 * atoms * channels * in_weight.shape[1],
    )


def layers(mesh):
    depths = {getattr(d, "coords", (0, 0, i))[2] for i, d in enumerate(mesh.devices[:, 0])}
    return len(depths)


def solution(mesh):
    placed = (
        P(both, None),
        P("space", None),
        P("kgrp", None),
        P("kgrp", None),
        P(),
        P(),
        P(),
        P(both, None),
        P(both, None),
        P(),
        P(),
        P(),
    )
    return jax.shard_map(
        functools.partial(local, layers(mesh)),
        mesh=mesh,
        in_specs=placed,
        out_specs=P(both, None),
        check_vma=False,
    )
```

```python
import functools
import math

import jax
import jax.numpy as jnp
import numpy as np
from jax import lax
from jax.experimental import pallas as pl
from jax.experimental.pallas import tpu as pltpu
from jax.sharding import PartitionSpec as P

box_side = 16.0
slab_step = 0.125
coord_rows = 16
bf16, f32 = jnp.bfloat16, jnp.float32

both = ("space", "kgrp")

vector_flops = 15000


def fit_cosine(degree):
    count = 64
    theta = (np.arange(count) + 0.5) * math.pi / count
    u = 0.125 * (1.0 + np.cos(theta))
    values = np.cos(2.0 * math.pi * np.sqrt(u))
    cheb = np.polynomial.chebyshev.Chebyshev.fit(u, values, degree, domain=[0.0, 0.25])
    return [float(c) for c in cheb.convert(kind=np.polynomial.Polynomial).coef]


cosine = fit_cosine(6)


def dot(a, b, dims):
    return lax.dot_general(a, b, (dims, ((), ())), preferred_element_type=f32)


def whole(count):
    return [pl.BlockSpec(memory_space=pltpu.VMEM)] * count


def call(body, outs, *args, flops=0, transcendentals=0):
    moved = sum(a.size * a.dtype.itemsize for a in (*args, *outs))
    return pl.pallas_call(
        body,
        out_shape=outs if len(outs) > 1 else outs[0],
        in_specs=whole(len(args)),
        out_specs=whole(len(outs)) if len(outs) > 1 else whole(1)[0],
        cost_estimate=pl.CostEstimate(
            flops=flops, bytes_accessed=moved, transcendentals=transcendentals
        ),
        compiler_params=pltpu.CompilerParams(vmem_limit_bytes=24 * 1024 * 1024),
    )(*args)


def shape(dims, dtype):
    return jax.ShapeDtypeStruct(dims, dtype)


def wave_share(inner):
    space = lax.axis_index("space")
    return (space ^ (space // inner & 1)) & (inner - 1)


def layer_member(members):
    member = lax.axis_index("space") * lax.axis_size("kgrp") + lax.axis_index("kgrp")
    return member & (members - 1)


def pack(features, positions, groups, slab_length):
    atoms, channels = features.shape
    row = lax.broadcasted_iota(jnp.int32, (coord_rows, atoms), 0)
    scale = jnp.where(row % 3 == 2, 1.0 / slab_length, 1.0 / box_side)
    rows = [features]
    for i in range(groups):
        own = positions[i * atoms : (i + 1) * atoms].T
        turns = jnp.pad(jnp.concatenate([own, own, own], axis=0), ((0, coord_rows - 9), (0, 0))) * scale
        high = lax.reduce_precision(turns, 8, 7)
        rest = turns - high
        middle = lax.reduce_precision(rest, 8, 7)
        parts = jnp.where(row < 3, high, jnp.where(row < 6, middle, rest - middle))
        parts = jnp.where(row < 9, parts, jnp.where(row == 9, 1.0, 0.0))
        rows.append(parts.astype(bf16))
    return jnp.concatenate(rows, axis=0)


def fill_phases(block_ref, waves, groups, phase_ref):
    group = lax.axis_index("kgrp")
    atoms = phase_ref.shape[0] // groups
    for i in range(groups):
        row = pl.multiple_of(atoms + (group ^ i) * coord_rows, coord_rows)
        turns = dot(block_ref[pl.ds(row, coord_rows), :], waves, ((0,), (0,)))
        part = turns - jnp.round(turns)
        u = part * part
        value = jnp.full_like(u, cosine[-1])
        for c in cosine[-2::-1]:
            value = value * u + c
        phase_ref[i * atoms : (i + 1) * atoms, :] = value.astype(bf16)


def prepare_body(inner, groups, index_ref, block_ref, wave_ref, phase_ref):
    share = index_ref.shape[1] // inner
    own = wave_share(inner)
    counts = index_ref[...].astype(f32)
    halves = []
    for which in (own, own ^ 1):
        mine = counts[:, :share]
        for i in range(1, inner):
            mine = jnp.where(which == i, counts[:, i * share : (i + 1) * share], mine)
        halves += [mine, mine]
    counts = jnp.concatenate(halves, axis=1)
    column = lax.broadcasted_iota(jnp.int32, (1, 4 * share), 1)
    cosines = (column < share) | ((column >= 2 * share) & (column < 3 * share))
    quarter = jnp.where(cosines, 0.0, -0.25)
    zeros = jnp.zeros((coord_rows - 10, 4 * share), f32)
    waves = jnp.concatenate([counts, counts, counts, quarter, zeros], axis=0)
    wave_ref[...] = waves.astype(bf16)
    fill_phases(block_ref, wave_ref[...], groups, phase_ref)


def phase_body(groups, block_ref, wave_ref, phase_ref):
    fill_phases(block_ref, wave_ref[...], groups, phase_ref)


def features_body(block_ref, out_ref):
    out_ref[...] = block_ref[: out_ref.shape[0], :]


def add_blocks(block_refs, phase_ref, first, atoms, total):
    for i, ref in enumerate(block_refs, first):
        phase = phase_ref[i * atoms : (i + 1) * atoms, :]
        term = dot(ref[:atoms, :], phase, ((0,), (0,)))
        total = term if total is None else total + term
    return total


def structure_body(blocks, atoms, *refs):
    block_refs, (phase_ref, *carry_refs, sum_ref) = refs[:blocks], refs[blocks:]
    total = carry_refs[0][...] if carry_refs else None
    sum_ref[...] = add_blocks(block_refs, phase_ref, 0, atoms, total)


def stack(ref, total):
    channels = ref.shape[1]
    for i in range(total.shape[1] // channels):
        part = total[:, i * channels : (i + 1) * channels]
        ref[i * channels : (i + 1) * channels, :] = part.astype(ref.dtype)


def split_body(atoms, members, groups, masks, *refs):
    block_ref, phase_ref, carry_ref, *far_refs, end_ref, keep_ref, send_ref = refs
    total = add_blocks([block_ref], phase_ref, groups - 1, atoms, carry_ref[...])
    columns = total.shape[1] // 2
    stack(keep_ref, total[:, :columns])
    stack(send_ref, total[:, columns:])
    halo = atoms // 4
    sums = keep_ref.shape[0] - halo
    other = layer_member(members) ^ groups
    even = (other & 1) == 0

    def beside(ref):
        return jnp.where(even, ref[atoms - halo : atoms, :], ref[:halo, :])

    keep_ref[sums:, :] = jnp.zeros_like(keep_ref[sums:, :])
    send_ref[sums : sums + halo, :] = beside(end_ref)
    needed = beside(far_refs[0])
    for mask, ref in zip(masks[1:], far_refs[1:]):
        needed = jnp.where(reaches(other, even, mask), beside(ref), needed)
    send_ref[sums + halo :, :] = needed


def reaches(member, even, mask):
    start = jnp.where(even, member, member + 1)
    return (start & mask) == (mask + 1) // 2


def mix_body(scale, a_ref, b_ref, mix_ref, filter_ref, y_ref):
    channels, columns = y_ref.shape
    tiles = [
        a_ref[i : i + channels, :].astype(f32) + b_ref[i : i + channels, :].astype(f32)
        for i in range(0, columns, channels)
    ]
    amps = (jnp.concatenate(tiles, axis=1) * scale).astype(bf16)
    half = amps.shape[1] // 2
    straight = dot(mix_ref[0], amps, ((0,), (0,)))
    crossed = dot(mix_ref[1], amps, ((0,), (0,)))
    crossed = jnp.concatenate([-crossed[:, half:], crossed[:, :half]], axis=1)
    y_ref[...] = (filter_ref[...] * (straight + crossed)).astype(bf16)


def near_body(phases, *refs):
    phase_refs, (y_ref, out_ref) = refs[:phases], refs[phases:]
    row = 0
    for ref in phase_refs:
        rows = ref.shape[0]
        out_ref[row : row + rows, :] = dot(ref[:, : y_ref.shape[1]], y_ref[...], ((1,), (1,)))
        row += rows


def far_body(phases, inv_scale, *refs):
    phase_refs, (y_ref, near_ref, *out_refs) = refs[:phases], refs[phases:]
    row = 0
    atoms = out_refs[0].shape[0]
    for ref in phase_refs:
        term = dot(ref[:, y_ref.shape[1] :], y_ref[...], ((1,), (1,)))
        for i in range(ref.shape[0] // atoms):
            block = term[i * atoms : (i + 1) * atoms] + near_ref[row : row + atoms, :]
            out = out_refs[row // atoms]
            out[...] = (block * inv_scale).astype(out.dtype)
            row += atoms


def hold_body(count, *refs):
    for a, b in zip(refs[:count], refs[count + 1 :]):
        b[...] = a[...]


def message_body(members, groups, masks, stages, *refs):
    feat_ref, *refs = refs
    near_refs, refs = refs[: len(masks)], refs[len(masks) :]
    core_ref, *refs = refs
    stage_refs, refs = refs[:stages], refs[stages:]
    msg_ref, width_ref, dist_ref, nbr_ref, base_ref = refs
    atoms, channels = dist_ref.shape[1], feat_ref.shape[1]
    features = feat_ref[:atoms, :]
    halo = atoms // 4
    member = layer_member(members)
    even = (member & 1) == 0
    layer = lax.axis_index("space") // (members // groups)

    def edge_of(ref):
        return ref[ref.shape[0] - halo :, :]

    start = jnp.where(even, layer, layer + 1)
    across = None
    for i, ref in enumerate(stage_refs):
        edge = edge_of(ref)
        across = edge if i == 0 else jnp.where((start & ((1 << i) - 1)) == 0, edge, across)
    far = edge_of(core_ref)
    ends = (member == 0) | (member == members - 1)
    if not stages:
        across = jnp.where(even, near_refs[-1][atoms - halo : atoms, :], near_refs[-1][:halo, :])
    far = jnp.where(ends, across, far)
    for mask, ref in zip(masks[1:], near_refs[1:]):
        rows = jnp.where(even, ref[atoms - halo : atoms, :], ref[:halo, :])
        far = jnp.where(reaches(member, even, mask), rows, far)
    beside = near_refs[0]
    before = jnp.where(even, far, beside[atoms - halo : atoms, :])
    after = jnp.where(even, beside[:halo, :], far)
    extended = jnp.concatenate([before, features, after], axis=0)
    projected = dot(msg_ref[...], extended, ((0,), (1,))).astype(bf16)
    row = lax.broadcasted_iota(jnp.int32, (extended.shape[0], atoms), 0)
    inverse = -1.0 / jnp.broadcast_to(width_ref[...], (atoms, channels)).T
    message = jnp.zeros((channels, atoms), f32)
    for j in range(nbr_ref.shape[0]):
        chosen = jnp.where(row == nbr_ref[j : j + 1, :], 1.0, 0.0).astype(bf16)
        nearby = dot(projected, chosen, ((1,), (0,)))
        message = message + jnp.exp(dist_ref[j : j + 1, :] * inverse) * nearby
    base_ref[...] = features.astype(f32) + message.T


def final_body(peers, *refs):
    base_ref, *refs = refs
    peer_refs, (gain_ref, in_ref, out_ref, result_ref) = refs[:peers], refs[peers:]
    mixed = base_ref[...]
    for ref in peer_refs:
        mixed = mixed + ref[...].astype(f32)
    inverse = lax.rsqrt(jnp.mean(mixed * mixed, axis=1, keepdims=True) + 1e-06)
    normed = (mixed * inverse * gain_ref[...]).astype(bf16)
    hidden = dot(normed, in_ref[...], ((1,), (0,)))
    half = 0.5 * hidden
    hidden = (half + half * jnp.tanh(half)).astype(bf16)
    result_ref[...] = (mixed + dot(hidden, out_ref[...], ((1,), (0,)))).astype(bf16)


def local(
    outer,
    features,
    positions,
    wave_index,
    wave_filter,
    mix_pair,
    msg_weight,
    chan_width,
    pair_dist,
    neighbours,
    norm_gain,
    in_weight,
    out_weight,
):
    atoms, channels = features.shape
    groups, space = lax.axis_size("kgrp"), lax.axis_size("space")
    inner = space // outer
    members = inner * groups
    devices = space * groups
    total_atoms = atoms * devices
    slab_length = total_atoms * slab_step
    share = wave_index.shape[0] // inner
    columns = 2 * share
    own_rows = groups * atoms

    def swap(x, mask):
        return lax.ppermute(x, both, [(i, i ^ mask) for i in range(devices)])

    bases = []
    for i in range(inner // 2):
        bases.append((2 * i + i.bit_count() % 2) * groups)
    near = [m + i for m in bases for i in range(groups)]
    block = {0: features}
    packed = pack(features, positions, groups, slab_length)
    source = packed
    for m in sorted(near[1:], key=lambda m: (m % groups != 0, m > groups)):
        block[m] = swap(source, m)
        source = call(
            features_body, (shape((atoms, channels), bf16),), source, flops=vector_flops * 300000
        )
    waves, own_phase = call(
        functools.partial(prepare_body, inner, groups),
        (shape((coord_rows, 2 * columns), bf16), shape((own_rows, 2 * columns), bf16)),
        wave_index.T,
        packed,
        flops=vector_flops * 2 * own_rows * columns,
    )
    phase = [own_phase]
    for m in bases[1:]:
        phase.append(
            call(
                functools.partial(phase_body, groups),
                (shape((own_rows, 2 * columns), bf16),),
                block[m],
                waves,
                flops=vector_flops * own_rows * columns,
            )
        )

    work = 4 * own_rows * columns * channels
    phase = lax.optimization_barrier(phase)
    part = None
    for m, rows in zip(bases, phase):
        members_here = [m + i for i in range(groups) if m + i != near[-1]]
        part = call(
            functools.partial(structure_body, len(members_here), atoms),
            (shape((channels, 2 * columns), f32),),
            *[block[i] if i else packed for i in members_here],
            rows,
            *([] if part is None else [part]),
            flops=work,
        )
    chain = [(2 << i) - 1 for i in range(members.bit_length() - 1)]
    far_masks = [m for m in reversed(chain) if m not in near]
    height = columns + atoms // 4
    keep, send = call(
        functools.partial(split_body, atoms, members, groups, far_masks),
        (shape((height, channels), f32), shape((height + atoms // 4, channels), bf16)),
        block[near[-1]],
        phase[-1],
        part,
        *[block[m ^ groups] for m in far_masks],
        block[members - 1],
        flops=work,
    )
    arrived = swap(send, groups)
    amps = (keep + arrived[:height].astype(f32)).astype(bf16)

    stages = []
    sums = lax.broadcasted_iota(jnp.int32, amps.shape, 0) < columns
    while (1 << len(stages)) < outer:
        if stages:
            both_sums = amps.astype(f32) + stages[-1].astype(f32)
            amps = jnp.where(sums, both_sums, amps.astype(f32)).astype(bf16)
        stages.append(swap(amps, ((2 << len(stages)) - 1) * members ^ groups))
    other = stages[-1] if stages else jnp.zeros_like(amps)
    held = (
        msg_weight,
        chan_width.reshape(1, channels),
        pair_dist.T,
        neighbours.T,
        norm_gain.reshape(1, channels),
        in_weight,
        out_weight,
    )
    held = call(
        functools.partial(hold_body, len(held)),
        tuple(shape(x.shape, x.dtype) for x in held),
        *held,
        amps,
        flops=2 * 10**9,
    )
    other, held = lax.optimization_barrier((other, held))
    msg_weight, chan_width, pair_dist, neighbours, norm_gain, in_weight, out_weight = held

    first = wave_share(inner) * share
    filters = lax.dynamic_slice_in_dim(wave_filter, first, share, 0).T
    filters = jnp.concatenate([filters, filters], axis=1)
    y = call(
        functools.partial(mix_body, 1.0 / math.sqrt(total_atoms)),
        (shape((channels, columns), bf16),),
        amps,
        other,
        mix_pair,
        filters,
        flops=4 * channels * channels * columns,
    )
    y_far = swap(y, groups)
    work = 2 * len(near) * atoms * channels * columns
    near_terms = call(
        functools.partial(near_body, len(phase)),
        (shape((len(near) * atoms, channels), f32),),
        *phase,
        y,
        flops=work,
    )
    terms = call(
        functools.partial(far_body, len(phase), 1.0 / math.sqrt(wave_index.shape[0] * groups)),
        tuple(shape((atoms, channels), bf16 if m else f32) for m in near),
        *phase,
        y_far,
        near_terms,
        flops=work,
    )
    peers = [terms[0]]
    for m in sorted(near[1:], key=lambda m: -(m & ~groups).bit_count()):
        peers.append(swap(terms[near.index(m)], m))

    near_masks = [m for m in chain if m in near]
    base = call(
        functools.partial(message_body, members, groups, near_masks, len(stages)),
        (shape((atoms, channels), f32),),
        packed,
        *[block[m] for m in near_masks],
        arrived,
        *stages,
        msg_weight,
        chan_width,
        pair_dist,
        neighbours,
        flops=vector_flops * atoms * neighbours.shape[0] * channels // 2,
        transcendentals=atoms * neighbours.shape[0] * channels,
    )
    return call(
        functools.partial(final_body, len(peers)),
        (shape((atoms, channels), bf16),),
        base,
        *peers,
        norm_gain,
        in_weight,
        out_weight,
        flops=4 * atoms * channels * in_weight.shape[1],
    )


def layers(mesh):
    depths = {getattr(d, "coords", (0, 0, i))[2] for i, d in enumerate(mesh.devices[:, 0])}
    return len(depths)


def solution(mesh):
    placed = (
        P(both, None),
        P("space", None),
        P("kgrp", None),
        P("kgrp", None),
        P(),
        P(),
        P(),
        P(both, None),
        P(both, None),
        P(),
        P(),
        P(),
    )
    return jax.shard_map(
        functools.partial(local, layers(mesh)),
        mesh=mesh,
        in_specs=placed,
        out_specs=P(both, None),
        check_vma=False,
    )
```

```python
import functools
import math

import jax
import jax.numpy as jnp
import numpy as np
from jax import lax
from jax.experimental import pallas as pl
from jax.experimental.pallas import tpu as pltpu
from jax.sharding import PartitionSpec as P

box_side = 16.0
slab_step = 0.125
coord_rows = 16
bf16, f32 = jnp.bfloat16, jnp.float32

both = ("space", "kgrp")

vector_flops = 15000


def fit_cosine(degree):
    count = 64
    theta = (np.arange(count) + 0.5) * math.pi / count
    u = 0.125 * (1.0 + np.cos(theta))
    values = np.cos(2.0 * math.pi * np.sqrt(u))
    cheb = np.polynomial.chebyshev.Chebyshev.fit(u, values, degree, domain=[0.0, 0.25])
    return [float(c) for c in cheb.convert(kind=np.polynomial.Polynomial).coef]


cosine = fit_cosine(6)


def dot(a, b, dims):
    return lax.dot_general(a, b, (dims, ((), ())), preferred_element_type=f32)


def whole(count):
    return [pl.BlockSpec(memory_space=pltpu.VMEM)] * count


def call(body, outs, *args, flops=0, transcendentals=0):
    moved = sum(a.size * a.dtype.itemsize for a in (*args, *outs))
    return pl.pallas_call(
        body,
        out_shape=outs if len(outs) > 1 else outs[0],
        in_specs=whole(len(args)),
        out_specs=whole(len(outs)) if len(outs) > 1 else whole(1)[0],
        cost_estimate=pl.CostEstimate(
            flops=flops, bytes_accessed=moved, transcendentals=transcendentals
        ),
        compiler_params=pltpu.CompilerParams(vmem_limit_bytes=24 * 1024 * 1024),
    )(*args)


def shape(dims, dtype):
    return jax.ShapeDtypeStruct(dims, dtype)


def wave_share(inner):
    space = lax.axis_index("space")
    return (space ^ (space // inner & 1)) & (inner - 1)


def layer_member(members):
    member = lax.axis_index("space") * lax.axis_size("kgrp") + lax.axis_index("kgrp")
    return member & (members - 1)


def pack(features, positions, groups, slab_length):
    atoms, channels = features.shape
    row = lax.broadcasted_iota(jnp.int32, (coord_rows, atoms), 0)
    scale = jnp.where(row % 3 == 2, 1.0 / slab_length, 1.0 / box_side)
    rows = [features]
    for i in range(groups):
        own = positions[i * atoms : (i + 1) * atoms].T
        turns = jnp.pad(jnp.concatenate([own, own, own], axis=0), ((0, coord_rows - 9), (0, 0))) * scale
        high = lax.reduce_precision(turns, 8, 7)
        rest = turns - high
        middle = lax.reduce_precision(rest, 8, 7)
        parts = jnp.where(row < 3, high, jnp.where(row < 6, middle, rest - middle))
        parts = jnp.where(row < 9, parts, jnp.where(row == 9, 1.0, 0.0))
        rows.append(parts.astype(bf16))
    return jnp.concatenate(rows, axis=0)


def fill_phases(block_ref, waves, groups, phase_ref):
    group = lax.axis_index("kgrp")
    atoms = phase_ref.shape[0] // groups
    for i in range(groups):
        row = pl.multiple_of(atoms + (group ^ i) * coord_rows, coord_rows)
        turns = dot(block_ref[pl.ds(row, coord_rows), :], waves, ((0,), (0,)))
        part = turns - jnp.round(turns)
        u = part * part
        value = jnp.full_like(u, cosine[-1])
        for c in cosine[-2::-1]:
            value = value * u + c
        phase_ref[i * atoms : (i + 1) * atoms, :] = value.astype(bf16)


def prepare_body(inner, groups, index_ref, block_ref, wave_ref, phase_ref):
    share = index_ref.shape[1] // inner
    own = wave_share(inner)
    counts = index_ref[...].astype(f32)
    halves = []
    for which in (own, own ^ 1):
        mine = counts[:, :share]
        for i in range(1, inner):
            mine = jnp.where(which == i, counts[:, i * share : (i + 1) * share], mine)
        halves += [mine, mine]
    counts = jnp.concatenate(halves, axis=1)
    column = lax.broadcasted_iota(jnp.int32, (1, 4 * share), 1)
    cosines = (column < share) | ((column >= 2 * share) & (column < 3 * share))
    quarter = jnp.where(cosines, 0.0, -0.25)
    zeros = jnp.zeros((coord_rows - 10, 4 * share), f32)
    waves = jnp.concatenate([counts, counts, counts, quarter, zeros], axis=0)
    wave_ref[...] = waves.astype(bf16)
    fill_phases(block_ref, wave_ref[...], groups, phase_ref)


def phase_body(groups, block_ref, wave_ref, phase_ref):
    fill_phases(block_ref, wave_ref[...], groups, phase_ref)


def features_body(block_ref, out_ref):
    out_ref[...] = block_ref[: out_ref.shape[0], :]


def add_blocks(block_refs, phase_ref, first, atoms, total):
    for i, ref in enumerate(block_refs, first):
        phase = phase_ref[i * atoms : (i + 1) * atoms, :]
        term = dot(ref[:atoms, :], phase, ((0,), (0,)))
        total = term if total is None else total + term
    return total


def structure_body(blocks, atoms, *refs):
    block_refs, (phase_ref, *carry_refs, sum_ref) = refs[:blocks], refs[blocks:]
    total = carry_refs[0][...] if carry_refs else None
    sum_ref[...] = add_blocks(block_refs, phase_ref, 0, atoms, total)


def stack(ref, total):
    channels = ref.shape[1]
    for i in range(total.shape[1] // channels):
        part = total[:, i * channels : (i + 1) * channels]
        ref[i * channels : (i + 1) * channels, :] = part.astype(ref.dtype)


def split_body(atoms, members, groups, masks, *refs):
    block_ref, phase_ref, carry_ref, *far_refs, end_ref, keep_ref, send_ref = refs
    total = add_blocks([block_ref], phase_ref, groups - 1, atoms, carry_ref[...])
    columns = total.shape[1] // 2
    stack(keep_ref, total[:, :columns])
    stack(send_ref, total[:, columns:])
    halo = atoms // 4
    sums = keep_ref.shape[0] - halo
    other = layer_member(members) ^ groups
    even = (other & 1) == 0

    def beside(ref):
        return jnp.where(even, ref[atoms - halo : atoms, :], ref[:halo, :])

    keep_ref[sums:, :] = jnp.zeros_like(keep_ref[sums:, :])
    send_ref[sums : sums + halo, :] = beside(end_ref)
    needed = beside(far_refs[0])
    for mask, ref in zip(masks[1:], far_refs[1:]):
        needed = jnp.where(reaches(other, even, mask), beside(ref), needed)
    send_ref[sums + halo :, :] = needed


def reaches(member, even, mask):
    start = jnp.where(even, member, member + 1)
    return (start & mask) == (mask + 1) // 2


def mix_body(scale, a_ref, b_ref, mix_ref, filter_ref, y_ref):
    channels, columns = y_ref.shape
    tiles = [
        a_ref[i : i + channels, :].astype(f32) + b_ref[i : i + channels, :].astype(f32)
        for i in range(0, columns, channels)
    ]
    amps = (jnp.concatenate(tiles, axis=1) * scale).astype(bf16)
    half = amps.shape[1] // 2
    straight = dot(mix_ref[0], amps, ((0,), (0,)))
    crossed = dot(mix_ref[1], amps, ((0,), (0,)))
    crossed = jnp.concatenate([-crossed[:, half:], crossed[:, :half]], axis=1)
    y_ref[...] = (filter_ref[...] * (straight + crossed)).astype(bf16)


def near_body(phases, *refs):
    phase_refs, (y_ref, out_ref) = refs[:phases], refs[phases:]
    row = 0
    for ref in phase_refs:
        rows = ref.shape[0]
        out_ref[row : row + rows, :] = dot(ref[:, : y_ref.shape[1]], y_ref[...], ((1,), (1,)))
        row += rows


def far_body(phases, inv_scale, *refs):
    phase_refs, (y_ref, near_ref, *out_refs) = refs[:phases], refs[phases:]
    row = 0
    atoms = out_refs[0].shape[0]
    for ref in phase_refs:
        term = dot(ref[:, y_ref.shape[1] :], y_ref[...], ((1,), (1,)))
        for i in range(ref.shape[0] // atoms):
            block = term[i * atoms : (i + 1) * atoms] + near_ref[row : row + atoms, :]
            out = out_refs[row // atoms]
            out[...] = (block * inv_scale).astype(out.dtype)
            row += atoms


def hold_body(count, *refs):
    for a, b in zip(refs[:count], refs[count + 1 :]):
        b[...] = a[...]


def message_body(members, groups, masks, stages, *refs):
    feat_ref, *refs = refs
    near_refs, refs = refs[: len(masks)], refs[len(masks) :]
    core_ref, *refs = refs
    stage_refs, refs = refs[:stages], refs[stages:]
    msg_ref, width_ref, dist_ref, nbr_ref, base_ref = refs
    atoms, channels = dist_ref.shape[1], feat_ref.shape[1]
    features = feat_ref[:atoms, :]
    halo = atoms // 4
    member = layer_member(members)
    even = (member & 1) == 0
    layer = lax.axis_index("space") // (members // groups)

    def edge_of(ref):
        return ref[ref.shape[0] - halo :, :]

    start = jnp.where(even, layer, layer + 1)
    across = None
    for i, ref in enumerate(stage_refs):
        edge = edge_of(ref)
        across = edge if i == 0 else jnp.where((start & ((1 << i) - 1)) == 0, edge, across)
    far = edge_of(core_ref)
    ends = (member == 0) | (member == members - 1)
    if not stages:
        across = jnp.where(even, near_refs[-1][atoms - halo : atoms, :], near_refs[-1][:halo, :])
    far = jnp.where(ends, across, far)
    for mask, ref in zip(masks[1:], near_refs[1:]):
        rows = jnp.where(even, ref[atoms - halo : atoms, :], ref[:halo, :])
        far = jnp.where(reaches(member, even, mask), rows, far)
    beside = near_refs[0]
    before = jnp.where(even, far, beside[atoms - halo : atoms, :])
    after = jnp.where(even, beside[:halo, :], far)
    extended = jnp.concatenate([before, features, after], axis=0)
    projected = dot(msg_ref[...], extended, ((0,), (1,))).astype(bf16)
    row = lax.broadcasted_iota(jnp.int32, (extended.shape[0], atoms), 0)
    inverse = -1.0 / jnp.broadcast_to(width_ref[...], (atoms, channels)).T
    message = jnp.zeros((channels, atoms), f32)
    for j in range(nbr_ref.shape[0]):
        chosen = jnp.where(row == nbr_ref[j : j + 1, :], 1.0, 0.0).astype(bf16)
        nearby = dot(projected, chosen, ((1,), (0,)))
        message = message + jnp.exp(dist_ref[j : j + 1, :] * inverse) * nearby
    base_ref[...] = features.astype(f32) + message.T


def final_body(peers, *refs):
    base_ref, *refs = refs
    peer_refs, (gain_ref, in_ref, out_ref, result_ref) = refs[:peers], refs[peers:]
    mixed = base_ref[...]
    for ref in peer_refs:
        mixed = mixed + ref[...].astype(f32)
    inverse = lax.rsqrt(jnp.mean(mixed * mixed, axis=1, keepdims=True) + 1e-06)
    normed = (mixed * inverse * gain_ref[...]).astype(bf16)
    hidden = dot(normed, in_ref[...], ((1,), (0,)))
    half = 0.5 * hidden
    hidden = (half + half * jnp.tanh(half)).astype(bf16)
    result_ref[...] = (mixed + dot(hidden, out_ref[...], ((1,), (0,)))).astype(bf16)


def local(
    outer,
    features,
    positions,
    wave_index,
    wave_filter,
    mix_pair,
    msg_weight,
    chan_width,
    pair_dist,
    neighbours,
    norm_gain,
    in_weight,
    out_weight,
):
    atoms, channels = features.shape
    groups, space = lax.axis_size("kgrp"), lax.axis_size("space")
    inner = space // outer
    members = inner * groups
    devices = space * groups
    total_atoms = atoms * devices
    slab_length = total_atoms * slab_step
    share = wave_index.shape[0] // inner
    columns = 2 * share
    own_rows = groups * atoms

    def swap(x, mask):
        return lax.ppermute(x, both, [(i, i ^ mask) for i in range(devices)])

    bases = []
    for i in range(inner // 2):
        bases.append((2 * i + i.bit_count() % 2) * groups)
    near = [m + i for m in bases for i in range(groups)]
    block = {0: features}
    packed = pack(features, positions, groups, slab_length)
    source = packed
    for m in sorted(near[1:], key=lambda m: (m % groups != 0, m > groups)):
        block[m] = swap(source, m)
        source = call(
            features_body, (shape((atoms, channels), bf16),), source, flops=vector_flops * 300000
        )
    waves, own_phase = call(
        functools.partial(prepare_body, inner, groups),
        (shape((coord_rows, 2 * columns), bf16), shape((own_rows, 2 * columns), bf16)),
        wave_index.T,
        packed,
        flops=vector_flops * 2 * own_rows * columns,
    )
    phase = [own_phase]
    for m in bases[1:]:
        phase.append(
            call(
                functools.partial(phase_body, groups),
                (shape((own_rows, 2 * columns), bf16),),
                block[m],
                waves,
                flops=vector_flops * own_rows * columns,
            )
        )

    work = 4 * own_rows * columns * channels
    phase = lax.optimization_barrier(phase)
    part = None
    for m, rows in zip(bases, phase):
        members_here = [m + i for i in range(groups) if m + i != near[-1]]
        part = call(
            functools.partial(structure_body, len(members_here), atoms),
            (shape((channels, 2 * columns), f32),),
            *[block[i] if i else packed for i in members_here],
            rows,
            *([] if part is None else [part]),
            flops=work,
        )
    chain = [(2 << i) - 1 for i in range(members.bit_length() - 1)]
    far_masks = [m for m in reversed(chain) if m not in near]
    height = columns + atoms // 4
    keep, send = call(
        functools.partial(split_body, atoms, members, groups, far_masks),
        (shape((height, channels), f32), shape((height + atoms // 4, channels), bf16)),
        block[near[-1]],
        phase[-1],
        part,
        *[block[m ^ groups] for m in far_masks],
        block[members - 1],
        flops=work,
    )
    arrived = swap(send, groups)
    amps = (keep + arrived[:height].astype(f32)).astype(bf16)

    stages = []
    sums = lax.broadcasted_iota(jnp.int32, amps.shape, 0) < columns
    while (1 << len(stages)) < outer:
        if stages:
            both_sums = amps.astype(f32) + stages[-1].astype(f32)
            amps = jnp.where(sums, both_sums, amps.astype(f32)).astype(bf16)
        stages.append(swap(amps, (outer >> len(stages)) * members - members ^ groups))
    other = stages[-1] if stages else jnp.zeros_like(amps)
    stages = stages[::-1]
    held = (
        msg_weight,
        chan_width.reshape(1, channels),
        pair_dist.T,
        neighbours.T,
        norm_gain.reshape(1, channels),
        in_weight,
        out_weight,
    )
    held = call(
        functools.partial(hold_body, len(held)),
        tuple(shape(x.shape, x.dtype) for x in held),
        *held,
        amps,
        flops=2 * 10**9,
    )
    other, held = lax.optimization_barrier((other, held))
    msg_weight, chan_width, pair_dist, neighbours, norm_gain, in_weight, out_weight = held

    first = wave_share(inner) * share
    filters = lax.dynamic_slice_in_dim(wave_filter, first, share, 0).T
    filters = jnp.concatenate([filters, filters], axis=1)
    y = call(
        functools.partial(mix_body, 1.0 / math.sqrt(total_atoms)),
        (shape((channels, columns), bf16),),
        amps,
        other,
        mix_pair,
        filters,
        flops=4 * channels * channels * columns,
    )
    y_far = swap(y, groups)
    work = 2 * len(near) * atoms * channels * columns
    near_terms = call(
        functools.partial(near_body, len(phase)),
        (shape((len(near) * atoms, channels), f32),),
        *phase,
        y,
        flops=work,
    )
    terms = call(
        functools.partial(far_body, len(phase), 1.0 / math.sqrt(wave_index.shape[0] * groups)),
        tuple(shape((atoms, channels), bf16 if m else f32) for m in near),
        *phase,
        y_far,
        near_terms,
        flops=work,
    )
    peers = [terms[0]]
    for m in sorted(near[1:], key=lambda m: -(m & ~groups).bit_count()):
        peers.append(swap(terms[near.index(m)], m))

    near_masks = [m for m in chain if m in near]
    base = call(
        functools.partial(message_body, members, groups, near_masks, len(stages)),
        (shape((atoms, channels), f32),),
        packed,
        *[block[m] for m in near_masks],
        arrived,
        *stages,
        msg_weight,
        chan_width,
        pair_dist,
        neighbours,
        flops=vector_flops * atoms * neighbours.shape[0] * channels // 2,
        transcendentals=atoms * neighbours.shape[0] * channels,
    )
    return call(
        functools.partial(final_body, len(peers)),
        (shape((atoms, channels), bf16),),
        base,
        *peers,
        norm_gain,
        in_weight,
        out_weight,
        flops=4 * atoms * channels * in_weight.shape[1],
    )


def layers(mesh):
    depths = {getattr(d, "coords", (0, 0, i))[2] for i, d in enumerate(mesh.devices[:, 0])}
    return len(depths)


def solution(mesh):
    placed = (
        P(both, None),
        P("space", None),
        P("kgrp", None),
        P("kgrp", None),
        P(),
        P(),
        P(),
        P(both, None),
        P(both, None),
        P(),
        P(),
        P(),
    )
    return jax.shard_map(
        functools.partial(local, layers(mesh)),
        mesh=mesh,
        in_specs=placed,
        out_specs=P(both, None),
        check_vma=False,
    )
```

```python
import functools
import math

import jax
import jax.numpy as jnp
import numpy as np
from jax import lax
from jax.experimental import pallas as pl
from jax.experimental.pallas import tpu as pltpu
from jax.sharding import PartitionSpec as P

box_side = 16.0
slab_step = 0.125
coord_rows = 16
bf16, f32 = jnp.bfloat16, jnp.float32

both = ("space", "kgrp")

vector_flops = 15000


def fit_cosine(degree):
    count = 64
    theta = (np.arange(count) + 0.5) * math.pi / count
    u = 0.125 * (1.0 + np.cos(theta))
    values = np.cos(2.0 * math.pi * np.sqrt(u))
    cheb = np.polynomial.chebyshev.Chebyshev.fit(u, values, degree, domain=[0.0, 0.25])
    return [float(c) for c in cheb.convert(kind=np.polynomial.Polynomial).coef]


cosine = fit_cosine(5)


def dot(a, b, dims):
    return lax.dot_general(a, b, (dims, ((), ())), preferred_element_type=f32)


def whole(count):
    return [pl.BlockSpec(memory_space=pltpu.VMEM)] * count


def call(body, outs, *args, flops=0, transcendentals=0):
    moved = sum(a.size * a.dtype.itemsize for a in (*args, *outs))
    return pl.pallas_call(
        body,
        out_shape=outs if len(outs) > 1 else outs[0],
        in_specs=whole(len(args)),
        out_specs=whole(len(outs)) if len(outs) > 1 else whole(1)[0],
        cost_estimate=pl.CostEstimate(
            flops=flops, bytes_accessed=moved, transcendentals=transcendentals
        ),
        compiler_params=pltpu.CompilerParams(vmem_limit_bytes=24 * 1024 * 1024),
    )(*args)


def shape(dims, dtype):
    return jax.ShapeDtypeStruct(dims, dtype)


def wave_share(inner):
    space = lax.axis_index("space")
    return (space ^ (space // inner & 1)) & (inner - 1)


def layer_member(members):
    member = lax.axis_index("space") * lax.axis_size("kgrp") + lax.axis_index("kgrp")
    return member & (members - 1)


def pack(features, positions, groups, slab_length):
    atoms, channels = features.shape
    row = lax.broadcasted_iota(jnp.int32, (coord_rows, atoms), 0)
    scale = jnp.where(row % 3 == 2, 1.0 / slab_length, 1.0 / box_side)
    rows = [features]
    for i in range(groups):
        own = positions[i * atoms : (i + 1) * atoms].T
        turns = jnp.pad(jnp.concatenate([own, own, own], axis=0), ((0, coord_rows - 9), (0, 0))) * scale
        high = lax.reduce_precision(turns, 8, 7)
        rest = turns - high
        middle = lax.reduce_precision(rest, 8, 7)
        parts = jnp.where(row < 3, high, jnp.where(row < 6, middle, rest - middle))
        parts = jnp.where(row < 9, parts, jnp.where(row == 9, 1.0, 0.0))
        rows.append(parts.astype(bf16))
    return jnp.concatenate(rows, axis=0)


def fill_phases(block_ref, waves, groups, phase_ref):
    group = lax.axis_index("kgrp")
    atoms = phase_ref.shape[0] // groups
    for i in range(groups):
        row = pl.multiple_of(atoms + (group ^ i) * coord_rows, coord_rows)
        turns = dot(block_ref[pl.ds(row, coord_rows), :], waves, ((0,), (0,)))
        part = turns - jnp.round(turns)
        u = part * part
        value = jnp.full_like(u, cosine[-1])
        for c in cosine[-2::-1]:
            value = value * u + c
        phase_ref[i * atoms : (i + 1) * atoms, :] = value.astype(bf16)


def prepare_body(inner, groups, index_ref, block_ref, wave_ref, phase_ref):
    share = index_ref.shape[1] // inner
    own = wave_share(inner)
    counts = index_ref[...].astype(f32)
    halves = []
    for which in (own, own ^ 1):
        mine = counts[:, :share]
        for i in range(1, inner):
            mine = jnp.where(which == i, counts[:, i * share : (i + 1) * share], mine)
        halves += [mine, mine]
    counts = jnp.concatenate(halves, axis=1)
    column = lax.broadcasted_iota(jnp.int32, (1, 4 * share), 1)
    cosines = (column < share) | ((column >= 2 * share) & (column < 3 * share))
    quarter = jnp.where(cosines, 0.0, -0.25)
    zeros = jnp.zeros((coord_rows - 10, 4 * share), f32)
    waves = jnp.concatenate([counts, counts, counts, quarter, zeros], axis=0)
    wave_ref[...] = waves.astype(bf16)
    fill_phases(block_ref, wave_ref[...], groups, phase_ref)


def phase_body(groups, block_ref, wave_ref, phase_ref):
    fill_phases(block_ref, wave_ref[...], groups, phase_ref)


def features_body(block_ref, out_ref):
    out_ref[...] = block_ref[: out_ref.shape[0], :]


def add_blocks(block_refs, phase_ref, total):
    atoms = phase_ref.shape[0] // len(block_refs)
    for i, ref in enumerate(block_refs):
        phase = phase_ref[i * atoms : (i + 1) * atoms, :]
        term = dot(ref[:atoms, :], phase, ((0,), (0,)))
        total = term if total is None else total + term
    return total


def structure_body(*refs):
    *block_refs, phase_ref, sum_ref = refs
    sum_ref[...] = add_blocks(block_refs, phase_ref, None)


def stack(ref, total):
    channels = ref.shape[1]
    for i in range(total.shape[1] // channels):
        part = total[:, i * channels : (i + 1) * channels]
        ref[i * channels : (i + 1) * channels, :] = part.astype(ref.dtype)


def split_body(blocks, members, groups, masks, *refs):
    block_refs, refs = refs[:blocks], refs[blocks:]
    phase_ref, carry_ref, *far_refs, end_ref, keep_ref, send_ref = refs
    total = add_blocks(block_refs, phase_ref, carry_ref[...])
    columns = total.shape[1] // 2
    stack(keep_ref, total[:, :columns])
    stack(send_ref, total[:, columns:])
    atoms = phase_ref.shape[0] // blocks
    halo = atoms // 4
    sums = keep_ref.shape[0] - halo
    other = layer_member(members) ^ groups
    even = (other & 1) == 0

    def beside(ref):
        return jnp.where(even, ref[atoms - halo : atoms, :], ref[:halo, :])

    keep_ref[sums:, :] = jnp.zeros_like(keep_ref[sums:, :])
    send_ref[sums : sums + halo, :] = beside(end_ref)
    needed = beside(far_refs[0])
    for mask, ref in zip(masks[1:], far_refs[1:]):
        needed = jnp.where(reaches(other, even, mask), beside(ref), needed)
    send_ref[sums + halo :, :] = needed


def reaches(member, even, mask):
    start = jnp.where(even, member, member + 1)
    return (start & mask) == (mask + 1) // 2


def mix_body(scale, a_ref, b_ref, mix_ref, filter_ref, y_ref):
    channels, columns = y_ref.shape
    tiles = [
        a_ref[i : i + channels, :].astype(f32) + b_ref[i : i + channels, :].astype(f32)
        for i in range(0, columns, channels)
    ]
    amps = (jnp.concatenate(tiles, axis=1) * scale).astype(bf16)
    half = amps.shape[1] // 2
    straight = dot(mix_ref[0], amps, ((0,), (0,)))
    crossed = dot(mix_ref[1], amps, ((0,), (0,)))
    crossed = jnp.concatenate([-crossed[:, half:], crossed[:, :half]], axis=1)
    y_ref[...] = (filter_ref[...] * (straight + crossed)).astype(bf16)


def near_body(phases, *refs):
    phase_refs, (y_ref, out_ref) = refs[:phases], refs[phases:]
    row = 0
    for ref in phase_refs:
        rows = ref.shape[0]
        out_ref[row : row + rows, :] = dot(ref[:, : y_ref.shape[1]], y_ref[...], ((1,), (1,)))
        row += rows


def far_body(phases, inv_scale, *refs):
    phase_refs, (y_ref, near_ref, *out_refs) = refs[:phases], refs[phases:]
    row = 0
    atoms = out_refs[0].shape[0]
    for ref in phase_refs:
        term = dot(ref[:, y_ref.shape[1] :], y_ref[...], ((1,), (1,)))
        for i in range(ref.shape[0] // atoms):
            block = term[i * atoms : (i + 1) * atoms] + near_ref[row : row + atoms, :]
            out = out_refs[row // atoms]
            out[...] = (block * inv_scale).astype(out.dtype)
            row += atoms


def hold_body(count, *refs):
    for a, b in zip(refs[:count], refs[count + 1 :]):
        b[...] = a[...]


def message_body(members, groups, masks, stages, *refs):
    feat_ref, *refs = refs
    near_refs, refs = refs[: len(masks)], refs[len(masks) :]
    core_ref, *refs = refs
    stage_refs, refs = refs[:stages], refs[stages:]
    msg_ref, width_ref, dist_ref, nbr_ref, base_ref = refs
    atoms, channels = dist_ref.shape[1], feat_ref.shape[1]
    features = feat_ref[:atoms, :]
    halo = atoms // 4
    member = layer_member(members)
    even = (member & 1) == 0
    layer = lax.axis_index("space") // (members // groups)

    def edge_of(ref):
        return ref[ref.shape[0] - halo :, :]

    start = jnp.where(even, layer, layer + 1)
    across = None
    for i, ref in enumerate(stage_refs):
        edge = edge_of(ref)
        across = edge if i == 0 else jnp.where((start & ((1 << i) - 1)) == 0, edge, across)
    far = edge_of(core_ref)
    ends = (member == 0) | (member == members - 1)
    if not stages:
        across = jnp.where(even, near_refs[-1][atoms - halo : atoms, :], near_refs[-1][:halo, :])
    far = jnp.where(ends, across, far)
    for mask, ref in zip(masks[1:], near_refs[1:]):
        rows = jnp.where(even, ref[atoms - halo : atoms, :], ref[:halo, :])
        far = jnp.where(reaches(member, even, mask), rows, far)
    beside = near_refs[0]
    before = jnp.where(even, far, beside[atoms - halo : atoms, :])
    after = jnp.where(even, beside[:halo, :], far)
    extended = jnp.concatenate([before, features, after], axis=0)
    projected = dot(msg_ref[...], extended, ((0,), (1,))).astype(bf16)
    row = lax.broadcasted_iota(jnp.int32, (extended.shape[0], atoms), 0)
    inverse = -1.0 / jnp.broadcast_to(width_ref[...], (atoms, channels)).T
    message = jnp.zeros((channels, atoms), f32)
    for j in range(nbr_ref.shape[0]):
        chosen = jnp.where(row == nbr_ref[j : j + 1, :], 1.0, 0.0).astype(bf16)
        nearby = dot(projected, chosen, ((1,), (0,)))
        message = message + jnp.exp(dist_ref[j : j + 1, :] * inverse) * nearby
    base_ref[...] = features.astype(f32) + message.T


def final_body(peers, *refs):
    base_ref, *refs = refs
    peer_refs, (gain_ref, in_ref, out_ref, result_ref) = refs[:peers], refs[peers:]
    mixed = base_ref[...]
    for ref in peer_refs:
        mixed = mixed + ref[...].astype(f32)
    inverse = lax.rsqrt(jnp.mean(mixed * mixed, axis=1, keepdims=True) + 1e-06)
    normed = (mixed * inverse * gain_ref[...]).astype(bf16)
    hidden = dot(normed, in_ref[...], ((1,), (0,)))
    half = 0.5 * hidden
    hidden = (half + half * jnp.tanh(half)).astype(bf16)
    result_ref[...] = (mixed + dot(hidden, out_ref[...], ((1,), (0,)))).astype(bf16)


def local(
    outer,
    features,
    positions,
    wave_index,
    wave_filter,
    mix_pair,
    msg_weight,
    chan_width,
    pair_dist,
    neighbours,
    norm_gain,
    in_weight,
    out_weight,
):
    atoms, channels = features.shape
    groups, space = lax.axis_size("kgrp"), lax.axis_size("space")
    inner = space // outer
    members = inner * groups
    devices = space * groups
    total_atoms = atoms * devices
    slab_length = total_atoms * slab_step
    share = wave_index.shape[0] // inner
    columns = 2 * share
    own_rows = groups * atoms

    def swap(x, mask):
        return lax.ppermute(x, both, [(i, i ^ mask) for i in range(devices)])

    bases = []
    for i in range(inner // 2):
        bases.append((2 * i + i.bit_count() % 2) * groups)
    near = [m + i for m in bases for i in range(groups)]
    block = {0: features}
    packed = pack(features, positions, groups, slab_length)
    source = packed
    for m in sorted(near[1:], key=lambda m: (m % groups != 0, m > groups)):
        block[m] = swap(source, m)
        source = call(
            features_body, (shape((atoms, channels), bf16),), source, flops=vector_flops * 300000
        )
    waves, own_phase = call(
        functools.partial(prepare_body, inner, groups),
        (shape((coord_rows, 2 * columns), bf16), shape((own_rows, 2 * columns), bf16)),
        wave_index.T,
        packed,
        flops=vector_flops * 2 * own_rows * columns,
    )
    phase = [own_phase]
    for m in bases[1:]:
        phase.append(
            call(
                functools.partial(phase_body, groups),
                (shape((own_rows, 2 * columns), bf16),),
                block[m],
                waves,
                flops=vector_flops * own_rows * columns,
            )
        )

    work = 4 * own_rows * columns * channels
    part = None
    for m, rows in zip(bases[:-1], phase[:-1]):
        here = call(
            structure_body,
            (shape((channels, 2 * columns), f32),),
            *[block[m + i] if m + i else packed for i in range(groups)],
            rows,
            flops=work,
        )
        part = here if part is None else part + here
    chain = [(2 << i) - 1 for i in range(members.bit_length() - 1)]
    far_masks = [m for m in reversed(chain) if m not in near]
    height = columns + atoms // 4
    keep, send = call(
        functools.partial(split_body, groups, members, groups, far_masks),
        (shape((height, channels), f32), shape((height + atoms // 4, channels), bf16)),
        *[block[bases[-1] + i] for i in range(groups)],
        phase[-1],
        part,
        *[block[m ^ groups] for m in far_masks],
        block[members - 1],
        flops=work,
    )
    arrived = swap(send, groups)
    amps = (keep + arrived[:height].astype(f32)).astype(bf16)

    stages = []
    sums = lax.broadcasted_iota(jnp.int32, amps.shape, 0) < columns
    while (1 << len(stages)) < outer:
        if stages:
            both_sums = amps.astype(f32) + stages[-1].astype(f32)
            amps = jnp.where(sums, both_sums, amps.astype(f32)).astype(bf16)
        stages.append(swap(amps, ((2 << len(stages)) - 1) * members ^ groups))
    other = stages[-1] if stages else jnp.zeros_like(amps)
    held = (
        msg_weight,
        chan_width.reshape(1, channels),
        pair_dist.T,
        neighbours.T,
        norm_gain.reshape(1, channels),
        in_weight,
        out_weight,
    )
    held = call(
        functools.partial(hold_body, len(held)),
        tuple(shape(x.shape, x.dtype) for x in held),
        *held,
        amps,
        flops=2 * 10**9,
    )
    other, held = lax.optimization_barrier((other, held))
    msg_weight, chan_width, pair_dist, neighbours, norm_gain, in_weight, out_weight = held

    first = wave_share(inner) * share
    filters = lax.dynamic_slice_in_dim(wave_filter, first, share, 0).T
    filters = jnp.concatenate([filters, filters], axis=1)
    y = call(
        functools.partial(mix_body, 1.0 / math.sqrt(total_atoms)),
        (shape((channels, columns), bf16),),
        amps,
        other,
        mix_pair,
        filters,
        flops=4 * channels * channels * columns,
    )
    y_far = swap(y, groups)
    work = 2 * len(near) * atoms * channels * columns
    near_terms = call(
        functools.partial(near_body, len(phase)),
        (shape((len(near) * atoms, channels), f32),),
        *phase,
        y,
        flops=work,
    )
    terms = call(
        functools.partial(far_body, len(phase), 1.0 / math.sqrt(wave_index.shape[0] * groups)),
        tuple(shape((atoms, channels), bf16 if m else f32) for m in near),
        *phase,
        y_far,
        near_terms,
        flops=work,
    )
    peers = [terms[0]]
    for m in sorted(near[1:], key=lambda m: -(m & ~groups).bit_count()):
        peers.append(swap(terms[near.index(m)], m))

    near_masks = [m for m in chain if m in near]
    base = call(
        functools.partial(message_body, members, groups, near_masks, len(stages)),
        (shape((atoms, channels), f32),),
        packed,
        *[block[m] for m in near_masks],
        arrived,
        *stages,
        msg_weight,
        chan_width,
        pair_dist,
        neighbours,
        flops=3 * channels * atoms * neighbours.shape[0] * atoms,
        transcendentals=atoms * neighbours.shape[0] * channels,
    )
    return call(
        functools.partial(final_body, len(peers)),
        (shape((atoms, channels), bf16),),
        base,
        *peers,
        norm_gain,
        in_weight,
        out_weight,
        flops=4 * atoms * channels * in_weight.shape[1],
    )


def layers(mesh):
    depths = {getattr(d, "coords", (0, 0, i))[2] for i, d in enumerate(mesh.devices[:, 0])}
    return len(depths)


def solution(mesh):
    placed = (
        P(both, None),
        P("space", None),
        P("kgrp", None),
        P("kgrp", None),
        P(),
        P(),
        P(),
        P(both, None),
        P(both, None),
        P(),
        P(),
        P(),
    )
    return jax.shard_map(
        functools.partial(local, layers(mesh)),
        mesh=mesh,
        in_specs=placed,
        out_specs=P(both, None),
        check_vma=False,
    )
```
